32 devices in a mesh: groups: 2 (over y), blk: 4 (over z), win: 4 (over x, core).
Axes of the slice: x: 2, y: 2, z: 4, core: 2. Of those that a mesh axis runs over, the one named last changes fastest.
Arguments:
- spectra: bfloat16 [2, 24, 1024, 201], P(None, 'win', ('groups', 'blk')), parts along dimension 2
- channel_slot: int32 [1024], P(('groups', 'blk')), parts along dimension 0, may hold values from 0 to 511, as said below
- partners: int32 [2, 4], replicated, may hold values from 0 to 3, as said below
Outputs:
- correlations: bfloat16 [2, 1024, 101, 128], P(None, ('groups', 'blk', 'win')), parts along dimension 1
The draws below stay inside these ranges and needn't reach their ends.
There are 2 independent parts, one for each index of `groups`. The reference program is written for one: setup_inputs(seed, part) draws one part's arguments, and reference() takes and returns one part's arrays. A program takes and returns all parts, laid end to end along the dimension named above; an argument that names none is the same for every part. Nothing has to cross between parts.
Inputs may be any that keep to these rules, and one draw needn't show every extreme that they name: channel_slot is a permutation of 0 to 511. For every acquisition shard s (channels s * 128 to s * 128 + 127) and every block b, exactly 32 of the shard's channels go to block b, and they take the slots b * 128 + s * 32 + q for q from 0 to 31. In round r, partners[r, i] = i XOR m_r for one value m_r of 1 to 3 per round; the rounds' values differ.
All inputs are finite; a program needn't handle non-finite values.
Results may differ from the reference program's by a relative error of at most 0.0057.
Values may be sent and summed in bfloat16 or wider, within the bound.
No kernel may reach another device: no remote copies, remote signals or barrier semaphores. Data moves between devices by JAX's collectives and lax.ppermute only.
A program may use at most 128 MiB of HBM per device.

```python
import math
import jax
import jax.numpy as jnp
from jax import lax

CH = 128
F = 201
L = 101
ROUNDS = 2
NB = 4
CHANNEL_COUNT = 512
WINDOW_COUNT = 24


def draw_spectra(key, part):
    noise_key = jax.random.fold_in(key, 11)
    transient_event_key = jax.random.fold_in(key, 12)
    colour_key = jax.random.fold_in(key, 13)
    gain_key = jax.random.fold_in(key, 15)
    linear_trend = 3.0 ** (jnp.arange(WINDOW_COUNT, dtype=jnp.float32) / (WINDOW_COUNT - 1))
    transient_event = jnp.exp(jax.random.uniform(transient_event_key, (WINDOW_COUNT, CHANNEL_COUNT), jnp.float32, -math.log(2.0), math.log(2.0)))
    spectral_tint = jnp.exp(jax.random.uniform(colour_key, (CHANNEL_COUNT, F), jnp.float32, math.log(0.3), math.log(3.0)))
    channel_gain = jnp.exp(jax.random.uniform(gain_key, (CHANNEL_COUNT,), jnp.float32, 0.0, math.log(10.0)))
    background_noise = jax.random.normal(noise_key, (2, WINDOW_COUNT, CHANNEL_COUNT, F), jnp.float32)
    value_array = background_noise * linear_trend[None, :, None, None] * transient_event[None, :, :, None] * spectral_tint[None, None, :, :]
    value_array = value_array * channel_gain[None, None, :, None]
    return value_array.astype(jnp.bfloat16)


def draw_channel_slot(key, part):
    per_peer = CH // NB
    keys = jax.random.split(jax.random.fold_in(key, 21), NB)
    orders = jax.vmap(lambda k: jax.random.permutation(k, CH))(keys).astype(jnp.int32)
    shard = jnp.arange(NB, dtype=jnp.int32)[:, None]
    block = orders % NB
    place = orders // NB
    slot = block * CH + shard * per_peer + place
    return slot.reshape(NB * CH).astype(jnp.int32)


def draw_partners(key, part):
    masks = jax.random.permutation(jax.random.fold_in(key, 31), NB - 1)[:ROUNDS].astype(jnp.int32) + 1
    index = jnp.arange(NB, dtype=jnp.int32)
    return jnp.bitwise_xor(index[None, :], masks[:, None]).astype(jnp.int32)


def setup_inputs(seed: int = 0, part: int = 0) -> dict:
    key_of = jax.random.split(jax.random.key(seed), 4)
    part_keys = jax.random.split(jax.random.fold_in(key_of[3], part), 4)
    return {
        "spectra": draw_spectra(jax.random.fold_in(jax.random.fold_in(key_of[3], part), 71), part),
        "channel_slot": draw_channel_slot(jax.random.fold_in(jax.random.fold_in(key_of[3], part), 71), part),
        "partners": draw_partners(jax.random.fold_in(key_of[3], 71), part),
    }


eps_power = 1e-06
half_band = 2

def band_mean(power, windows):
    nbins = power.shape[1]
    padded = jnp.pad(power, ((0, 0), (half_band, half_band)))
    ones = jnp.pad(jnp.ones((nbins,), jnp.float32), (half_band, half_band))
    total = padded[:, 0:nbins]
    count = ones[0:nbins]
    for offset in range(1, 2 * half_band + 1):
        total = total + padded[:, offset:offset + nbins]
        count = count + ones[offset:offset + nbins]
    return total / (count * windows)

def whiten(parts, power, windows):
    scale = lax.rsqrt(band_mean(power, windows) + eps_power)
    return (parts.astype(jnp.float32) * scale).astype(jnp.bfloat16)

def lag_table(nbins, nlags, windows):
    samples = 2 * (nbins - 1)
    freq = jnp.arange(nbins, dtype=jnp.int32)
    lags = jnp.arange(nlags, dtype=jnp.int32) - (nlags - 1) // 2
    phase_index = freq[:, None] * lags[None, :] % samples
    angle = 2.0 * math.pi / samples * phase_index.astype(jnp.float32)
    weight = jnp.where((freq == 0) | (freq == nbins - 1), 1.0, 2.0).astype(jnp.float32)
    norm = 1.0 / math.sqrt(windows * samples)
    cos_part = weight[:, None] * jnp.cos(angle) * norm
    sin_part = -weight[:, None] * jnp.sin(angle) * norm
    return jnp.concatenate([cos_part, sin_part], axis=0)

def correlate(sources, receivers, table):
    left = jnp.concatenate([sources[0], sources[1]], axis=0).astype(jnp.float32)
    turned = jnp.concatenate([sources[1], -sources[0]], axis=0).astype(jnp.float32)
    right = jnp.concatenate([receivers[0], receivers[1]], axis=0).astype(jnp.float32)
    tile = 32
    count = left.shape[1] // tile

    def one_tile(index):
        start = index * tile
        part_left = lax.dynamic_slice_in_dim(left, start, tile, 1)
        part_turned = lax.dynamic_slice_in_dim(turned, start, tile, 1)
        real = jnp.einsum('wak,wbk->kab', part_left, right, precision=lax.Precision.HIGHEST)
        imag = jnp.einsum('wak,wbk->kab', part_turned, right, precision=lax.Precision.HIGHEST)
        stacked = jnp.concatenate([real, imag], axis=0)
        return jnp.einsum('kab,kl->alb', stacked, table, precision=lax.Precision.HIGHEST)
    result = lax.map(one_tile, jnp.arange(count, dtype=jnp.int32))
    return result.reshape(count * tile, table.shape[1], right.shape[1]).astype(jnp.bfloat16)

def reference(spectra, channel_slot, partners):
    blocked = jnp.zeros_like(spectra).at[:, :, channel_slot, :].set(spectra)
    value_array = blocked.astype(jnp.float32)
    power = lax.optimization_barrier(jnp.sum(value_array * value_array, axis=(0, 1)))
    white = whiten(blocked, power, WINDOW_COUNT)
    grouped = white.reshape(2, WINDOW_COUNT, NB, CH, F)
    table = lag_table(F, L, WINDOW_COUNT)
    rounds = []
    for round_index in range(ROUNDS):

        def per_block(index):
            own = lax.dynamic_index_in_dim(grouped, index, 2, keepdims=False)
            other = lax.dynamic_index_in_dim(grouped, partners[round_index, index].astype(jnp.int32), 2, keepdims=False)
            return correlate(own, other, table)
        result = lax.map(per_block, jnp.arange(NB, dtype=jnp.int32))
        rounds.append(result.reshape(NB * CH, L, CH))
    return jnp.stack(rounds, axis=0)
```

```python
import math

import jax
import jax.numpy as jnp
import numpy as np
from jax import lax
from jax.experimental import pallas as pl
from jax.experimental.pallas import tpu as pltpu
from jax.sharding import PartitionSpec as P

L = 101
ROUNDS = 2

eps_power = 1e-06
half_band = 2
tile_rows = 8
LANES = 128
K8 = 8
K16 = 16
VMEM_BYTES = 56 * 1024 * 1024


def shortened(value):

    def short(part):
        return part.astype(jnp.bfloat16) if part.dtype == jnp.float32 else part

    return jax.tree.map(short, value)


def partner(value, axis, distance):
    mask = 2**distance
    pairs = [(source, source ^ mask) for source in range(lax.axis_size(axis))]
    return lax.ppermute(value, axis, pairs)


def band_mean(power, windows):
    nbins = power.shape[1]
    padded = jnp.pad(power, ((0, 0), (half_band, half_band)))
    ones = jnp.pad(jnp.ones((nbins,), jnp.float32), (half_band, half_band))
    total = padded[:, 0:nbins]
    count = ones[0:nbins]
    for offset in range(1, 2 * half_band + 1):
        total = total + padded[:, offset : offset + nbins]
        count = count + ones[offset : offset + nbins]
    return total / (count * windows)


def power_of(parts):
    value_array = parts.astype(jnp.float32)
    return jnp.sum(value_array * value_array, axis=(0, 1))


def whiten(parts, power, windows):
    scale = lax.rsqrt(band_mean(power, windows) + eps_power)
    return (parts.astype(jnp.float32) * scale).astype(jnp.bfloat16)


def lag_table(nbins, nlags, windows):
    samples = 2 * (nbins - 1)
    freq = jnp.arange(nbins, dtype=jnp.int32)
    lags = jnp.arange(nlags, dtype=jnp.int32) - (nlags - 1) // 2
    phase_index = freq[:, None] * lags[None, :] % samples
    angle = 2.0 * math.pi / samples * phase_index.astype(jnp.float32)
    weight = jnp.where((freq == 0) | (freq == nbins - 1), 1.0, 2.0).astype(jnp.float32)
    norm = 1.0 / math.sqrt(windows * samples)
    cos_part = weight[:, None] * jnp.cos(angle) * norm
    sin_part = -weight[:, None] * jnp.sin(angle) * norm
    return jnp.concatenate([cos_part, sin_part], axis=0)


def correlate(sources, receivers, table):
    left = jnp.concatenate([sources[0], sources[1]], axis=0)
    turned = jnp.concatenate([sources[1], -sources[0]], axis=0)
    right = jnp.concatenate([receivers[0], receivers[1]], axis=0)
    count = left.shape[1] // tile_rows

    def one_tile(index):
        start = index * tile_rows
        part_left = lax.dynamic_slice_in_dim(left, start, tile_rows, 1)
        part_turned = lax.dynamic_slice_in_dim(turned, start, tile_rows, 1)
        real = jnp.einsum("wak,wbk->kab", part_left, right, preferred_element_type=jnp.float32)
        imag = jnp.einsum("wak,wbk->kab", part_turned, right, preferred_element_type=jnp.float32)
        stacked = jnp.concatenate([real, imag], axis=0)
        return jnp.einsum("kab,kl->alb", stacked, table, precision=lax.Precision.HIGHEST)

    result = lax.map(one_tile, jnp.arange(count, dtype=jnp.int32))
    return result.reshape(count * tile_rows, table.shape[1], right.shape[1]).astype(jnp.bfloat16)


def make_walker(mask_bits, depth):

    def walker(moving):
        for bit in range(depth):
            if mask_bits >> bit & 1:
                moving = jax.tree.map(
                    lambda part, own: part.astype(own.dtype),
                    partner(shortened(moving), "blk", bit),
                    moving,
                )
        return moving

    return walker


def walking_body(spectra, channel_slot, partners):
    n_blk = lax.axis_size("blk")
    n_win = lax.axis_size("win")
    chans = spectra.shape[2]
    nbins = spectra.shape[3]
    per_peer = chans // n_blk
    here = lax.axis_index("blk")
    target = channel_slot // chans * per_peer + channel_slot % chans - here * per_peer
    selector = (jnp.arange(chans, dtype=jnp.int32)[:, None] == target[None, :]).astype(jnp.bfloat16)
    ordered = jnp.einsum(
        "pc,rwcf->rwpf", selector, spectra, preferred_element_type=jnp.float32
    ).astype(jnp.bfloat16)
    blocked = lax.all_to_all(ordered, "blk", split_axis=2, concat_axis=2, tiled=True)
    windows = spectra.shape[1] * n_win
    power = lax.psum(power_of(blocked), "win")
    outgoing = whiten(blocked, power, windows)
    own_all = lax.all_gather(outgoing, "win", axis=1, tiled=True)
    share = chans // n_win
    sources = lax.dynamic_slice_in_dim(own_all, lax.axis_index("win") * share, share, 2)
    table = lag_table(nbins, L, windows)
    masks = jnp.bitwise_xor(partners[:, here], here)
    bits = n_blk.bit_length() - 1
    results = []
    walkers = [make_walker(mask_bits, bits) for mask_bits in range(1, n_blk)]
    for round_index in range(ROUNDS):
        moving = lax.switch(masks[round_index] - 1, walkers, outgoing)
        partner_all = jax.tree.map(
            lambda part, own: part.astype(own.dtype),
            lax.all_gather(shortened(moving), "win", axis=1, tiled=True),
            moving,
        )
        results.append(correlate(sources, partner_all, table))
    return jnp.stack(results, axis=0)


def iota(shape, dim):
    return lax.broadcasted_iota(jnp.int32, shape, dim)


def bins_of(nbins):
    return -(-nbins // K16)


def lag_matrix(nbins, windows):
    samples = 2 * (nbins - 1)
    groups = 2 * bins_of(nbins)
    rows = -(-L // K8) * K8
    freq = np.arange(nbins)
    lags = np.arange(L) - (L - 1) // 2
    angle = 2.0 * np.pi / samples * (freq[:, None] * lags[None, :] % samples)
    weight = np.where((freq == 0) | (freq == nbins - 1), 1.0, 2.0)[:, None] / math.sqrt(windows * samples)
    full = np.zeros((rows, 2, groups * K8))
    full[:L, 0, :nbins] = (weight * np.cos(angle)).T
    full[:L, 1, :nbins] = -(weight * np.sin(angle)).T
    full = full.reshape(rows, 2, groups, K8).transpose(0, 2, 1, 3).reshape(rows, groups * 2 * K8)
    high = full.astype(jnp.bfloat16)
    low = (full - high.astype(np.float64)).astype(jnp.bfloat16)
    return np.concatenate([high, low], axis=0)


def pack_kernel(layout, nbins, here_ref, part_ref, slot_ref, x_ref, *rest):
    outs, (wide_ref, blocks_ref) = rest[: len(layout)], rest[len(layout) :]
    n_blk, n_grp, n_row, lanes = blocks_ref.shape
    per_peer = lanes // 4
    chans = slot_ref.shape[1]
    pairs = n_row // K16
    here = here_ref[0]
    slot = slot_ref[...]
    target = slot // chans * per_peer + slot % chans - here * per_peer
    target = jnp.concatenate([target] * 4, axis=1)
    wide_ref[...] = jnp.zeros(wide_ref.shape, jnp.float32)
    shape = (lanes, 4 * chans)
    row, col = iota(shape, 0), iota(shape, 1)
    same = row // per_peer == col // chans
    for block in range(n_blk):
        pick = jnp.where(same & (target == block * per_peer + row % per_peer), 1.0, 0.0).astype(jnp.bfloat16)
        for pair in range(pairs):
            part = jnp.concatenate([x_ref[p, pl.ds(pair * 2 * chans, 2 * chans), :] for p in range(2)], axis=0)
            wide_ref[:, pl.ds(0, nbins)] = jnp.dot(pick, part, preferred_element_type=jnp.float32)
            turned = wide_ref[...].T[: n_grp * K16].astype(jnp.bfloat16)
            blocks_ref[block, :, pl.ds(pair * K16, K16), :] = turned.reshape(n_grp, K16, lanes)
    masks = [part_ref[r, here] ^ here for r in range(ROUNDS)]
    masks.append(masks[0] ^ masks[1])
    for out, message in zip(outs, layout):
        for place, (step, name) in enumerate(message):
            mask = 0 if name is None else masks[name]
            out[place] = blocks_ref[here ^ step ^ mask]


def scale_of(power_ref, nbins, windows):
    rows = power_ref.shape[0] - 2 * K8
    total = power_ref[pl.ds(K8 - half_band, rows), :]
    for offset in range(1, 2 * half_band + 1):
        total = total + power_ref[pl.ds(K8 - half_band + offset, rows), :]
    bin_ = iota(total.shape, 0)
    count = jnp.minimum(bin_ + half_band, nbins - 1) - jnp.maximum(bin_ - half_band, 0) + 1
    count = jnp.maximum(count, 1).astype(jnp.float32)
    return lax.rsqrt(total / (count * windows) + eps_power)


def source_kernel(nbins, windows, *refs):
    src, (out_ref, power_ref, scale_ref) = refs[:4], refs[4:]
    n_grp, n_row, lanes = src[0].shape[1:]
    pairs = n_row // K16
    share = lanes // 4
    step = pl.program_id(0)

    @pl.when(step == 0)
    def _():
        total = jnp.zeros((n_grp, K16, lanes), jnp.float32)
        for ref in src:
            for pair in range(pairs):
                value = ref[0, :, pl.ds(pair * K16, K16), :].astype(jnp.float32)
                total = total + value * value
        total = total.reshape(n_grp * K16, lanes)
        total = total + pltpu.roll(total, 2 * share, 1)
        total = total + pltpu.roll(total, share, 1)
        power_ref[...] = jnp.zeros(power_ref.shape, jnp.float32)
        power_ref[pl.ds(K8, n_grp * K16), :] = total
        scale_ref[...] = scale_of(power_ref, nbins, windows).reshape(scale_ref.shape)

    scale = scale_ref[step]
    white = [
        [
            (ref[0, step, pl.ds(pair * K16, K16), :].astype(jnp.float32) * scale).astype(jnp.bfloat16).astype(jnp.float32)
            for ref in src
        ]
        for pair in range(pairs)
    ]
    lane_group = iota((share, lanes), 1) // (4 * K8)
    keep = iota((share, K8, lanes), 1) == iota((share, K8, lanes), 2) % K8
    for half in range(2):
        rows = [white[pair][e][half * K8 : (half + 1) * K8] for pair in range(pairs) for e in range(4)]
        rows = rows + [jnp.zeros((lanes - len(rows) * K8, lanes), jnp.float32)]
        turned = jnp.concatenate(rows, axis=0).T
        by_group = [turned[g * share : (g + 1) * share] for g in range(4)]
        crossed = [by_group[2], by_group[3], -by_group[0], -by_group[1]]
        for pair in range(pairs):
            spread = []
            for values in (by_group, crossed):
                line = jnp.zeros((share, lanes), jnp.float32)
                for g in range(4):
                    moved = values[g]
                    shift = (g - pair) * 4 * K8 % lanes
                    if shift:
                        moved = pltpu.roll(moved, shift, 1)
                    line = jnp.where(lane_group == g, moved, line)
                line = jnp.broadcast_to(line.reshape(share, 1, lanes), (share, K8, lanes))
                spread.append(jnp.where(keep, line, 0.0))
            both = jnp.concatenate(spread, axis=1).astype(jnp.bfloat16)
            out_ref[half, :, pl.ds(pair * lanes, lanes)] = both.reshape(share * 2 * K8, lanes)


def correlate_kernel(places, nbins, windows, here_ref, left_hbm, lag_ref, *rest):
    count = 1 + max(index for by_d in places for by_e in by_d for index, _ in by_e)
    pieces, rest = rest[:count], rest[count:]
    out_ref, left_ref, right_ref, cross_ref, power_ref, scale_ref, sem = rest
    copy = pltpu.make_async_copy(left_hbm, left_ref, sem)
    copy.start()
    n_grp, n_row, lanes = pieces[0].shape[1:]
    pairs = n_row // K16
    share = lanes // 4
    here = here_ref[0]
    shape = (4 * lanes, 4 * lanes)
    row, col = iota(shape, 0), iota(shape, 1)
    shard = (row // lanes) ^ here
    spot = row % lanes // share * lanes + shard * share + row % share
    order = jnp.where(col == spot, 1.0, 0.0).astype(jnp.bfloat16)
    power_ref[...] = jnp.zeros(power_ref.shape, jnp.float32)
    for r in range(ROUNDS):
        side = pl.ds(r * lanes, lanes)
        total = jnp.zeros((n_grp, 2, K8, lanes), jnp.float32)
        for e in range(4):
            parts = [pieces[places[r][d][e][0]][places[r][d][e][1]].reshape(n_grp * n_row, lanes) for d in range(4)]
            moved = jnp.dot(jnp.concatenate(parts, axis=1), order, preferred_element_type=jnp.float32)
            moved = moved.reshape(n_grp, pairs, 2, K8, 4 * lanes)
            for pair in range(pairs):
                for g in range(4):
                    value = moved[:, pair, :, :, g * lanes : (g + 1) * lanes]
                    right_ref[:, :, (pair * 4 + g) * 4 + e, :, side] = value
                    total = total + value * value
        power_ref[pl.ds(K8, n_grp * K16), side] = total.reshape(n_grp * K16, lanes)
    scale_ref[...] = scale_of(power_ref, nbins, windows).reshape(scale_ref.shape)
    copy.wait()

    def one_group(index, carry):
        for half in range(2):
            white = (right_ref[index, half] * scale_ref[index, half]).astype(jnp.bfloat16)
            white = white.reshape(-1, white.shape[-1])
            cross = jnp.dot(left_ref[2 * index + half], white, preferred_element_type=jnp.float32)
            place = pl.multiple_of((2 * index + half) * 2 * K8, 2 * K8)
            cross_ref[:, pl.ds(place, 2 * K8), :] = cross.astype(jnp.bfloat16).reshape(-1, 2 * K8, cross.shape[-1])
        return carry

    lax.fori_loop(0, n_grp, one_group, 0)

    def one_source(index, carry):
        both = jnp.dot(lag_ref[...], cross_ref[index], preferred_element_type=jnp.float32)
        rows = both.shape[0] // 2
        lagged = (both[:rows] + both[rows:])[:L].astype(jnp.bfloat16)
        for r in range(ROUNDS):
            out_ref[r, index] = lagged[:, r * lanes : (r + 1) * lanes]
        return carry

    lax.fori_loop(0, share, one_source, 0)


def swap(value, axis, mask):
    return lax.ppermute(value, axis, [(i, i ^ mask) for i in range(lax.axis_size(axis))])


def call(kernel, outs, operands, scratch, name, specs=None, **grid):
    return pl.pallas_call(
        kernel,
        out_shape=outs,
        in_specs=specs,
        scratch_shapes=scratch,
        compiler_params=pltpu.CompilerParams(vmem_limit_bytes=VMEM_BYTES),
        name=name,
        **grid,
    )(*operands)


def make_branch(case):
    near, far = (case, 1 - case) if case < 2 else (None, None)

    def branch(spectra, channel_slot, partners, here):
        chans, nbins = spectra.shape[2:]
        windows = spectra.shape[1] * lax.axis_size("win")
        n_grp = bins_of(nbins)
        pairs = spectra.shape[1] // 2
        share = chans // 4
        piece = (n_grp, pairs * K16, chans)
        win = lax.axis_index("win")
        if case < 2:
            far_first = [[(2, near)], [(2, None)], [(2, 2)], [(2, far)]]
        else:
            far_first = [[(2, 0), (2, 1)], [(3, None)], [(2, None)]]
        layout = far_first + [[(1, 0), (1, 1)], [(1, None)], [(0, 0), (0, 1)], [(0, None)]]
        vmem, smem = pl.BlockSpec(memory_space=pltpu.VMEM), pl.BlockSpec(memory_space=pltpu.SMEM)
        messages = call(
            lambda *refs: pack_kernel(layout, nbins, *refs),
            [jax.ShapeDtypeStruct((len(m),) + piece, jnp.bfloat16) for m in layout],
            (here, partners, channel_slot.reshape(1, chans), spectra.reshape(2, -1, nbins)),
            [pltpu.VMEM((chans, 2 * LANES), jnp.float32), pltpu.VMEM((4,) + piece, jnp.bfloat16)],
            "pack",
            [smem, smem, vmem, vmem],
        )
        far_sent, (near_sent, near_src, own, own_src) = messages[:-4], messages[-4:]
        far_got = [swap(m, "blk", 2) for m in far_sent]
        near_got = swap(near_sent, "blk", 1)
        near_src_got = swap(near_src, "blk", 1)
        if case < 2:
            relayed = [swap(far_got[i], "blk", 1) for i in (1, 0, 2)]
            src = [own_src, near_src_got, far_got[1], relayed[1]]
            held = {(far, 2): (far_got[3], 0), (near, 2): (far_got[0], 0)}
            held |= {(far, 3): (relayed[2], 0), (near, 3): (relayed[0], 0)}
        else:
            relayed = [swap(far_got[i], "blk", 1) for i in (0, 1)]
            src = [own_src, near_src_got, far_got[2], relayed[1]]
            held = {(r, 2): (far_got[0], r) for r in range(2)} | {(r, 3): (relayed[0], 1 - r) for r in range(2)}
        held |= {(r, 0): (own, r) for r in range(2)} | {(r, 1): (near_got, r) for r in range(2)}
        z = here[0]
        mine = (z >> 1) == (win >> 1)
        low = [jnp.where(mine, src[d], src[d + 2]) for d in range(2)]
        high = [jnp.where(mine, src[d + 2], src[d]) for d in range(2)]
        odd = ((win ^ z) & 1) == 1
        across = swap(jnp.concatenate(high, axis=0), "win", 2)
        first, second = low, [across[0:1], across[1:2]]
        sources = []
        for two in (first, second):
            sources.append(jnp.where(odd, two[1], two[0]))
            sources.append(swap(jnp.where(odd, two[0], two[1]), "win", 1))
        left = call(
            lambda *refs: source_kernel(nbins, windows, *refs),
            jax.ShapeDtypeStruct((2 * n_grp, share * 2 * K8, pairs * chans), jnp.bfloat16),
            sources,
            [
                pltpu.VMEM((n_grp * K16 + 2 * K8, chans), jnp.float32),
                pltpu.VMEM((n_grp, K16, chans), jnp.float32),
            ],
            "sources",
            [vmem] * 4,
            grid=(n_grp,),
            out_specs=pl.BlockSpec((2, share * 2 * K8, pairs * chans), lambda i: (i, 0, 0)),
        )
        pieces, places = [], [[[None] * 4 for _ in range(4)] for _ in range(ROUNDS)]
        gathered = {}
        for r in range(ROUNDS):
            for d in range(4):
                array, index = held[r, d]
                if id(array) not in gathered:
                    over = swap(array, "win", 2)
                    gathered[id(array)] = (len(pieces), array)
                    pieces += [array, swap(array, "win", 1), over, swap(over, "win", 1)]
                for e in range(4):
                    places[r][d][e] = (gathered[id(array)][0] + e, index)
        lag = jnp.asarray(lag_matrix(nbins, windows))
        return call(
            lambda *refs: correlate_kernel(places, nbins, windows, *refs),
            jax.ShapeDtypeStruct((ROUNDS, share, L, chans), jnp.bfloat16),
            (here, left, lag, *pieces),
            [
                pltpu.VMEM(left.shape, jnp.bfloat16),
                pltpu.VMEM((n_grp, 2, pairs * 16, K8, ROUNDS * chans), jnp.float32),
                pltpu.VMEM((share, n_grp * 4 * K8, ROUNDS * chans), jnp.bfloat16),
                pltpu.VMEM((n_grp * K16 + 2 * K8, ROUNDS * chans), jnp.float32),
                pltpu.VMEM((n_grp, 2, K8, ROUNDS * chans), jnp.float32),
                pltpu.SemaphoreType.DMA,
            ],
            "correlate",
            [smem, pl.BlockSpec(memory_space=pl.ANY)] + [vmem] * (1 + len(pieces)),
        )

    return branch


def gathering_body(spectra, channel_slot, partners):
    here = lax.axis_index("blk")
    masks = partners[:, here] ^ here
    case = jnp.where(masks[0] == 1, 0, jnp.where(masks[1] == 1, 1, 2))
    branches = [make_branch(i) for i in range(3)]
    return lax.switch(case, branches, spectra, channel_slot, partners, here.reshape(1))


def solution(mesh):
    in_specs = (P(None, "win", ("groups", "blk"), None), P(("groups", "blk")), P())
    out_specs = P(None, ("groups", "blk", "win"), None, None)

    def body(spectra, channel_slot, partners):
        small = all((mesh.shape[axis] - 1).bit_length() == 2 for axis in ("blk", "win"))
        small = small and spectra.shape[2] == LANES and spectra.shape[1] % 2 == 0 and spectra.shape[3] <= 2 * LANES
        return (gathering_body if small else walking_body)(spectra, channel_slot, partners)

    return jax.shard_map(body, mesh=mesh, in_specs=in_specs, out_specs=out_specs, check_vma=False)
```

```python
import math

import jax
import jax.numpy as jnp
import numpy as np
from jax import lax
from jax.experimental import pallas as pl
from jax.experimental.pallas import tpu as pltpu
from jax.sharding import PartitionSpec as P

L = 101
ROUNDS = 2

eps_power = 1e-06
half_band = 2
tile_rows = 8
LANES = 128
K8 = 8
K16 = 16
VMEM_BYTES = 56 * 1024 * 1024


def shortened(value):

    def short(part):
        return part.astype(jnp.bfloat16) if part.dtype == jnp.float32 else part

    return jax.tree.map(short, value)


def partner(value, axis, distance):
    mask = 2**distance
    pairs = [(source, source ^ mask) for source in range(lax.axis_size(axis))]
    return lax.ppermute(value, axis, pairs)


def band_mean(power, windows):
    nbins = power.shape[1]
    padded = jnp.pad(power, ((0, 0), (half_band, half_band)))
    ones = jnp.pad(jnp.ones((nbins,), jnp.float32), (half_band, half_band))
    total = padded[:, 0:nbins]
    count = ones[0:nbins]
    for offset in range(1, 2 * half_band + 1):
        total = total + padded[:, offset : offset + nbins]
        count = count + ones[offset : offset + nbins]
    return total / (count * windows)


def power_of(parts):
    value_array = parts.astype(jnp.float32)
    return jnp.sum(value_array * value_array, axis=(0, 1))


def whiten(parts, power, windows):
    scale = lax.rsqrt(band_mean(power, windows) + eps_power)
    return (parts.astype(jnp.float32) * scale).astype(jnp.bfloat16)


def lag_table(nbins, nlags, windows):
    samples = 2 * (nbins - 1)
    freq = jnp.arange(nbins, dtype=jnp.int32)
    lags = jnp.arange(nlags, dtype=jnp.int32) - (nlags - 1) // 2
    phase_index = freq[:, None] * lags[None, :] % samples
    angle = 2.0 * math.pi / samples * phase_index.astype(jnp.float32)
    weight = jnp.where((freq == 0) | (freq == nbins - 1), 1.0, 2.0).astype(jnp.float32)
    norm = 1.0 / math.sqrt(windows * samples)
    cos_part = weight[:, None] * jnp.cos(angle) * norm
    sin_part = -weight[:, None] * jnp.sin(angle) * norm
    return jnp.concatenate([cos_part, sin_part], axis=0)


def correlate(sources, receivers, table):
    left = jnp.concatenate([sources[0], sources[1]], axis=0)
    turned = jnp.concatenate([sources[1], -sources[0]], axis=0)
    right = jnp.concatenate([receivers[0], receivers[1]], axis=0)
    count = left.shape[1] // tile_rows

    def one_tile(index):
        start = index * tile_rows
        part_left = lax.dynamic_slice_in_dim(left, start, tile_rows, 1)
        part_turned = lax.dynamic_slice_in_dim(turned, start, tile_rows, 1)
        real = jnp.einsum("wak,wbk->kab", part_left, right, preferred_element_type=jnp.float32)
        imag = jnp.einsum("wak,wbk->kab", part_turned, right, preferred_element_type=jnp.float32)
        stacked = jnp.concatenate([real, imag], axis=0)
        return jnp.einsum("kab,kl->alb", stacked, table, precision=lax.Precision.HIGHEST)

    result = lax.map(one_tile, jnp.arange(count, dtype=jnp.int32))
    return result.reshape(count * tile_rows, table.shape[1], right.shape[1]).astype(jnp.bfloat16)


def make_walker(mask_bits, depth):

    def walker(moving):
        for bit in range(depth):
            if mask_bits >> bit & 1:
                moving = jax.tree.map(
                    lambda part, own: part.astype(own.dtype),
                    partner(shortened(moving), "blk", bit),
                    moving,
                )
        return moving

    return walker


def walking_body(spectra, channel_slot, partners):
    n_blk = lax.axis_size("blk")
    n_win = lax.axis_size("win")
    chans = spectra.shape[2]
    nbins = spectra.shape[3]
    per_peer = chans // n_blk
    here = lax.axis_index("blk")
    target = channel_slot // chans * per_peer + channel_slot % chans - here * per_peer
    selector = (jnp.arange(chans, dtype=jnp.int32)[:, None] == target[None, :]).astype(jnp.bfloat16)
    ordered = jnp.einsum(
        "pc,rwcf->rwpf", selector, spectra, preferred_element_type=jnp.float32
    ).astype(jnp.bfloat16)
    blocked = lax.all_to_all(ordered, "blk", split_axis=2, concat_axis=2, tiled=True)
    windows = spectra.shape[1] * n_win
    power = lax.psum(power_of(blocked), "win")
    outgoing = whiten(blocked, power, windows)
    own_all = lax.all_gather(outgoing, "win", axis=1, tiled=True)
    share = chans // n_win
    sources = lax.dynamic_slice_in_dim(own_all, lax.axis_index("win") * share, share, 2)
    table = lag_table(nbins, L, windows)
    masks = jnp.bitwise_xor(partners[:, here], here)
    bits = n_blk.bit_length() - 1
    results = []
    walkers = [make_walker(mask_bits, bits) for mask_bits in range(1, n_blk)]
    for round_index in range(ROUNDS):
        moving = lax.switch(masks[round_index] - 1, walkers, outgoing)
        partner_all = jax.tree.map(
            lambda part, own: part.astype(own.dtype),
            lax.all_gather(shortened(moving), "win", axis=1, tiled=True),
            moving,
        )
        results.append(correlate(sources, partner_all, table))
    return jnp.stack(results, axis=0)


def iota(shape, dim):
    return lax.broadcasted_iota(jnp.int32, shape, dim)


def bins_of(nbins):
    return -(-nbins // K16)


def lag_matrix(nbins):
    samples = 2 * (nbins - 1)
    groups = 2 * bins_of(nbins)
    rows = -(-L // K8) * K8
    freq = np.arange(nbins)
    lags = np.arange(L) - (L - 1) // 2
    angle = 2.0 * np.pi / samples * (freq[:, None] * lags[None, :] % samples)
    weight = np.where((freq == 0) | (freq == nbins - 1), 1.0, 2.0)[:, None]
    full = np.zeros((rows, 2, groups * K8))
    full[:L, 0, :nbins] = (weight * np.cos(angle)).T
    full[:L, 1, :nbins] = -(weight * np.sin(angle)).T
    full = full.reshape(rows, 2, groups, K8).transpose(0, 2, 1, 3).reshape(rows, groups * 2 * K8)
    return full.astype(jnp.bfloat16)


def pack_kernel(layout, nbins, here_ref, part_ref, slot_ref, x_ref, *rest):
    outs, (wide_ref, blocks_ref) = rest[: len(layout)], rest[len(layout) :]
    n_blk, n_grp, n_row, lanes = blocks_ref.shape
    per_peer = lanes // 4
    chans = slot_ref.shape[1]
    here = here_ref[0]
    slot = slot_ref[...]
    target = slot // chans * per_peer + slot % chans - here * per_peer
    shape = (n_blk * lanes, chans)
    row = iota(shape, 0)
    pick = jnp.where(target == row // lanes * per_peer + row % per_peer, 1.0, 0.0).astype(jnp.bfloat16)
    rows = math.prod(x_ref.shape[:-1])
    wide = lax.dot_general(x_ref[...].reshape(rows, chans), pick, (((1,), (1,)), ((), ())), preferred_element_type=jnp.float32)
    for block in range(n_blk):
        wide_ref[block, pl.ds(0, rows), :] = wide[:, block * lanes : (block + 1) * lanes]
    bins = n_grp * K16
    lane_group = iota((bins, lanes), 1) // per_peer
    inside = iota((bins, lanes), 0) < nbins
    for block in range(n_blk):
        for pair in range(n_row // K16):
            value = jnp.zeros((bins, lanes), jnp.float32)
            for g in range(4):
                start = (2 * pair + g % 2) * 2 * nbins + g // 2
                value = jnp.where(lane_group == g, wide_ref[block, pl.ds(start, bins, stride=2), :], value)
            value = jnp.where(inside, value, 0.0).astype(jnp.bfloat16)
            blocks_ref[block, :, pl.ds(pair * K16, K16), :] = value.reshape(n_grp, K16, lanes)
    masks = [part_ref[r, here] ^ here for r in range(ROUNDS)]
    masks.append(masks[0] ^ masks[1])
    for out, message in zip(outs, layout):
        for place, (step, name) in enumerate(message):
            mask = 0 if name is None else masks[name]
            out[place] = blocks_ref[here ^ step ^ mask]


def scale_of(power_ref, nbins, windows):
    rows = power_ref.shape[0] - 2 * K8
    total = power_ref[pl.ds(K8 - half_band, rows), :]
    for offset in range(1, 2 * half_band + 1):
        total = total + power_ref[pl.ds(K8 - half_band + offset, rows), :]
    bin_ = iota(total.shape, 0)
    count = jnp.minimum(bin_ + half_band, nbins - 1) - jnp.maximum(bin_ - half_band, 0) + 1
    count = jnp.maximum(count, 1).astype(jnp.float32)
    return lax.rsqrt(total / (count * windows) + eps_power)


def source_kernel(nbins, windows, *refs):
    src, (out_ref, power_ref, scale_ref) = refs[:4], refs[4:]
    n_grp, n_row, lanes = src[0].shape[1:]
    pairs = n_row // K16
    share = lanes // 4
    step = pl.program_id(0)

    @pl.when(step == 0)
    def _():
        total = jnp.zeros((n_grp, K16, lanes), jnp.float32)
        for ref in src:
            for pair in range(pairs):
                value = ref[0, :, pl.ds(pair * K16, K16), :].astype(jnp.float32)
                total = total + value * value
        total = total.reshape(n_grp * K16, lanes)
        total = total + pltpu.roll(total, 2 * share, 1)
        total = total + pltpu.roll(total, share, 1)
        power_ref[...] = jnp.zeros(power_ref.shape, jnp.float32)
        power_ref[pl.ds(K8, n_grp * K16), :] = total
        scale_ref[...] = scale_of(power_ref, nbins, windows).reshape(scale_ref.shape)

    scale = scale_ref[step]
    white = [
        [
            (ref[0, step, pl.ds(pair * K16, K16), :].astype(jnp.float32) * scale).astype(jnp.bfloat16).astype(jnp.float32)
            for ref in src
        ]
        for pair in range(pairs)
    ]
    lane_group = iota((share, lanes), 1) // (4 * K8)
    keep = iota((share, K8, lanes), 1) == iota((share, K8, lanes), 2) % K8
    for half in range(2):
        rows = [white[pair][e][half * K8 : (half + 1) * K8] for pair in range(pairs) for e in range(4)]
        rows = rows + [jnp.zeros((lanes - len(rows) * K8, lanes), jnp.float32)]
        turned = jnp.concatenate(rows, axis=0).T
        by_group = [turned[g * share : (g + 1) * share] for g in range(4)]
        crossed = [by_group[2], by_group[3], -by_group[0], -by_group[1]]
        for pair in range(pairs):
            spread = []
            for values in (by_group, crossed):
                line = jnp.zeros((share, lanes), jnp.float32)
                for g in range(4):
                    moved = values[g]
                    shift = (g - pair) * 4 * K8 % lanes
                    if shift:
                        moved = pltpu.roll(moved, shift, 1)
                    line = jnp.where(lane_group == g, moved, line)
                line = jnp.broadcast_to(line.reshape(share, 1, lanes), (share, K8, lanes))
                spread.append(jnp.where(keep, line, 0.0))
            both = jnp.concatenate(spread, axis=1).astype(jnp.bfloat16)
            out_ref[half, :, pl.ds(pair * lanes, lanes)] = both.reshape(share * 2 * K8, lanes)


def take_pieces(pieces, places, phase, here, right_ref, power_ref, scale_ref, nbins, windows):
    n_grp, n_row, lanes = pieces[0].shape[1:]
    pairs = n_row // K16
    share = lanes // 4
    shape = (4 * lanes, 4 * lanes)
    row, col = iota(shape, 0), iota(shape, 1)
    kind = row // lanes
    half = (here >> 1) ^ phase ^ (kind >> 1)
    odd = (here ^ kind) & 1
    spot = row % lanes // share * lanes + (2 * half + odd) * share + row % share
    order = jnp.where(col == spot, 1.0, 0.0).astype(jnp.bfloat16)
    total = jnp.zeros((n_grp, 2, K8, lanes), jnp.float32)
    for e in range(4):
        parts = [pieces[operand][index].reshape(n_grp * n_row, lanes) for operand, index in places[e]]
        moved = jnp.dot(jnp.concatenate(parts, axis=1), order, preferred_element_type=jnp.float32)
        moved = moved.reshape(n_grp, pairs, 2, K8, 4 * lanes)
        for pair in range(pairs):
            for g in range(4):
                value = moved[:, pair, :, :, g * lanes : (g + 1) * lanes]
                right_ref[:, :, (pair * 4 + g) * 4 + e] = value
                total = total + value * value
    power_ref[...] = jnp.zeros(power_ref.shape, jnp.float32)
    power_ref[pl.ds(K8, n_grp * K16), :] = total.reshape(n_grp * K16, lanes)
    scale_ref[...] = scale_of(power_ref, nbins, windows).reshape(scale_ref.shape)


def whitened(right_ref, scale_ref, index, half):
    white = (right_ref[index, half] * scale_ref[index, half]).astype(jnp.bfloat16)
    return white.reshape(-1, white.shape[-1])


def receive_kernel(places, nbins, windows, here_ref, *rest):
    pieces, (out_ref, right_ref, power_ref, scale_ref) = rest[:-4], rest[-4:]
    take_pieces(pieces, places, 0, here_ref[0], right_ref, power_ref, scale_ref, nbins, windows)

    def one_group(index, carry):
        for half in range(2):
            out_ref[2 * index + half] = whitened(right_ref, scale_ref, index, half)
        return carry

    lax.fori_loop(0, right_ref.shape[0], one_group, 0)


def correlate_kernel(places, nbins, windows, here_ref, left_hbm, early_hbm, lag_ref, *rest):
    pieces, rest = rest[:-9], rest[-9:]
    out_ref, left_ref, early_ref, right_ref, cross_ref, lagged_ref, power_ref, scale_ref, sems = rest
    copies = [
        pltpu.make_async_copy(left_hbm, left_ref, sems.at[0]),
        pltpu.make_async_copy(early_hbm, early_ref, sems.at[1]),
    ]
    for copy in copies:
        copy.start()
    here = here_ref[0]
    take_pieces(pieces, places, 1, here, right_ref, power_ref, scale_ref, nbins, windows)
    for copy in copies:
        copy.wait()

    def one_group(index, carry):
        for half in range(2):
            both = jnp.concatenate([early_ref[2 * index + half], whitened(right_ref, scale_ref, index, half)], axis=1)
            cross = jnp.dot(left_ref[2 * index + half], both, preferred_element_type=jnp.float32)
            place = pl.multiple_of((2 * index + half) * 2 * K8, 2 * K8)
            cross_ref[:, pl.ds(place, 2 * K8), :] = cross.astype(jnp.bfloat16).reshape(-1, 2 * K8, cross.shape[-1])
        return carry

    lax.fori_loop(0, right_ref.shape[0], one_group, 0)
    norm = 1.0 / math.sqrt(windows * 2 * (nbins - 1))
    share, lanes = cross_ref.shape[0], pieces[0].shape[-1]
    first = iota((lag_ref.shape[0], lanes), 1) // (2 * share) == here >> 1

    def one_source(index, carry):
        lagged = jnp.dot(lag_ref[...], cross_ref[index], preferred_element_type=jnp.float32) * norm
        early, late = lagged[:, :lanes], lagged[:, lanes:]
        rounds = [jnp.where(first, early, late), pltpu.roll(jnp.where(first, late, early), lanes // 2, 1)]
        for r in range(ROUNDS):
            lagged_ref[r, pl.ds(index, lagged.shape[0], stride=share), :] = rounds[r]
        return carry

    lax.fori_loop(0, share, one_source, 0, unroll=4)
    for r in range(ROUNDS):
        out_ref[r] = lagged_ref[r, pl.ds(0, L * share), :].astype(jnp.bfloat16).reshape(L, share, lanes)


def swap(value, axis, mask):
    return lax.ppermute(value, axis, [(i, i ^ mask) for i in range(lax.axis_size(axis))])


def call(kernel, outs, operands, scratch, name, specs=None, traffic=1000, **grid):
    return pl.pallas_call(
        kernel,
        cost_estimate=pl.CostEstimate(flops=0, bytes_accessed=traffic, transcendentals=0),
        out_shape=outs,
        in_specs=specs,
        scratch_shapes=scratch,
        compiler_params=pltpu.CompilerParams(vmem_limit_bytes=VMEM_BYTES),
        name=name,
        **grid,
    )(*operands)


def after(value, *earlier):
    return lax.optimization_barrier((value, *earlier))[0]


def make_branch(case):
    one, other = (case, 1 - case) if case < 2 else (None, None)

    def branch(spectra, channel_slot, partners, here):
        chans, nbins = spectra.shape[2:]
        windows = spectra.shape[1] * lax.axis_size("win")
        n_grp = bins_of(nbins)
        pairs = spectra.shape[1] // 2
        share = chans // 4
        piece = (n_grp, pairs * K16, chans)
        win = lax.axis_index("win")
        if case < 2:
            layout = [[(2, one), (2, None)], [(2, 2), (2, other)]]
        else:
            layout = [[(2, None), (3, None)], [(2, 0), (2, 1)]]
        layout += [[(1, 0), (1, 1), (1, None)], [(0, 0), (0, 1)], [(0, None)]]
        vmem, smem = pl.BlockSpec(memory_space=pltpu.VMEM), pl.BlockSpec(memory_space=pltpu.SMEM)
        far_a, far_b, near, own, own_src = call(
            lambda *refs: pack_kernel(layout, nbins, *refs),
            [jax.ShapeDtypeStruct((len(m),) + piece, jnp.bfloat16) for m in layout],
            (here, partners, channel_slot.reshape(1, chans), spectra.transpose(1, 3, 0, 2)),
            [
                pltpu.VMEM((4, spectra.shape[1] * 2 * nbins + 4 * K16, chans), jnp.float32),
                pltpu.VMEM((4,) + piece, jnp.bfloat16),
            ],
            "pack",
            [smem, smem, vmem, vmem],
        )
        z = here[0]
        mine = (z >> 1) == (win >> 1)
        got_1 = swap(near, "blk", 1)
        got_a = swap(far_a, "blk", 2)
        over_0 = swap(own, "win", 2)
        over_1 = swap(after(got_1[:2], over_0), "win", 2)
        got_b = swap(after(far_b, got_a), "blk", 2)
        core_2b = swap(got_b, "win", 1)
        if case < 2:
            got_3a = swap(got_a, "blk", 1)
            over_2a = swap(got_a[:1], "win", 2)
            got_3b = swap(after(got_b[:1], core_2b), "blk", 1)
            src = [own_src, got_1[2:], got_a[1:], after(got_3a[:1], over_1, over_2a)]
        else:
            got_3a = swap(got_a[1:], "blk", 1)
            got_3b = swap(after(got_b, core_2b), "blk", 1)
            src = [own_src, got_1[2:], got_a[:1], after(got_3a, over_1)]
        high = [jnp.where(mine, src[d + 2], src[d]) for d in range(2)]
        across = swap(jnp.concatenate(high, axis=0), "win", 2)
        low = [jnp.where(mine, src[d], src[d + 2]) for d in range(2)]
        if case < 2:
            over_2b = swap(got_b[1:], "win", 2)
            over_3a = swap(got_3a[1:], "win", 2)
            over_3b = None
            arrays = {
                "2a": [got_a, over_2a],
                "3a": [got_3a, over_3a],
                "2b": [got_b, over_2b],
                "3b": [got_3b, over_3b],
            }
            held = {(other, 2): ("2b", (1, 0)), (one, 2): ("2a", (0, 0))}
            held |= {(other, 3): ("3b", (0, 0)), (one, 3): ("3a", (1, 0))}
        else:
            over_2b = swap(got_b, "win", 2)
            over_3b = None
            arrays = {"2b": [got_b, over_2b], "3b": [got_3b, over_3b]}
            held = {(r, 2): ("2b", (r, r)) for r in range(2)} | {(r, 3): ("3b", (1 - r, 1 - r)) for r in range(2)}
        arrays |= {0: [own, over_0], 1: [got_1, over_1]}
        held |= {(r, d): (d, (r, r)) for r in range(2) for d in range(2)}
        def doubled(name, last=()):
            held_here, over = arrays[name]
            core_here = core_2b if name == "2b" else swap(held_here, "win", 1)
            arrays[name] = [held_here, core_here, over, swap(after(over, *last) if last else over, "win", 1)]

        def places_of(phase):
            names = list(dict.fromkeys(held[r, d][0] for r in range(ROUNDS) for d in (2 * phase, 2 * phase + 1)))
            places = [[] for _ in range(4)]
            for r in range(ROUNDS):
                for d in (2 * phase, 2 * phase + 1):
                    name, (whole, part) = held[r, d]
                    for e in range(4):
                        size = arrays[name][e].shape[0]
                        index = whole if size == arrays[name][0].shape[0] else part
                        places[e].append((4 * names.index(name) + e, index))
            return places, [array for name in names for array in arrays[name]]

        for name in (0, 1):
            doubled(name)
        lag = jnp.asarray(lag_matrix(nbins))
        taken = [
            pltpu.VMEM((n_grp, 2, pairs * 16, K8, chans), jnp.float32),
            pltpu.VMEM((n_grp * K16 + 2 * K8, chans), jnp.float32),
            pltpu.VMEM((n_grp, 2, K8, chans), jnp.float32),
        ]
        early_places, early_pieces = places_of(0)
        early = call(
            lambda *refs: receive_kernel(early_places, nbins, windows, *refs),
            jax.ShapeDtypeStruct((2 * n_grp, pairs * 16 * K8, chans), jnp.bfloat16),
            (here, *early_pieces),
            taken,
            "receivers",
            [smem] + [vmem] * len(early_pieces),
            traffic=12 * 2**20,
        )
        over_3b = swap(got_3b, "win", 2)
        across = after(across, got_3b, early)
        odd = ((win ^ z) & 1) == 1
        first, second = low, [across[0:1], across[1:2]]
        sources = []
        for two in (first, second):
            sources.append(jnp.where(odd, two[1], two[0]))
            sources.append(swap(jnp.where(odd, two[0], two[1]), "win", 1))
        left = call(
            lambda *refs: source_kernel(nbins, windows, *refs),
            jax.ShapeDtypeStruct((2 * n_grp, share * 2 * K8, pairs * chans), jnp.bfloat16),
            sources,
            [
                pltpu.VMEM((n_grp * K16 + 2 * K8, chans), jnp.float32),
                pltpu.VMEM((n_grp, K16, chans), jnp.float32),
            ],
            "sources",
            [vmem] * 4,
            traffic=20 * 2**20,
            grid=(n_grp,),
            out_specs=pl.BlockSpec((2, share * 2 * K8, pairs * chans), lambda i: (i, 0, 0)),
        )
        arrays["3b"] = [got_3b, over_3b]
        for name in list(arrays):
            if name not in (0, 1):
                doubled(name, [left] if name == "3b" else [])
        late_places, late_pieces = places_of(1)
        hbm = pl.BlockSpec(memory_space=pl.ANY)
        by_lag = call(
            lambda *refs: correlate_kernel(late_places, nbins, windows, *refs),
            jax.ShapeDtypeStruct((ROUNDS, L, share, chans), jnp.bfloat16),
            (here, left, early, lag, *late_pieces),
            [
                pltpu.VMEM(left.shape, jnp.bfloat16),
                pltpu.VMEM(early.shape, jnp.bfloat16),
                taken[0],
                pltpu.VMEM((share, n_grp * 4 * K8, ROUNDS * chans), jnp.bfloat16),
                pltpu.VMEM((ROUNDS, lag.shape[0] * share, chans), jnp.float32),
                *taken[1:],
                pltpu.SemaphoreType.DMA((2,)),
            ],
            "correlate",
            [smem, hbm, hbm] + [vmem] * (1 + len(late_pieces)),
        )
        return by_lag.transpose(0, 2, 1, 3)

    return branch


def gathering_body(spectra, channel_slot, partners):
    here = lax.axis_index("blk")
    masks = partners[:, 0]
    case = jnp.where(masks[0] == 1, 0, jnp.where(masks[1] == 1, 1, 2))
    branches = [make_branch(i) for i in range(3)]
    return lax.switch(case, branches, spectra, channel_slot, partners, here.reshape(1))


def solution(mesh):
    in_specs = (P(None, "win", ("groups", "blk"), None), P(("groups", "blk")), P())
    out_specs = P(None, ("groups", "blk", "win"), None, None)

    def body(spectra, channel_slot, partners):
        small = all((mesh.shape[axis] - 1).bit_length() == 2 for axis in ("blk", "win"))
        small = small and spectra.shape[2] == LANES and spectra.shape[1] % 2 == 0 and spectra.shape[3] <= 2 * LANES
        return (gathering_body if small else walking_body)(spectra, channel_slot, partners)

    return jax.shard_map(body, mesh=mesh, in_specs=in_specs, out_specs=out_specs, check_vma=False)
```

```python
import math

import jax
import jax.numpy as jnp
import numpy as np
from jax import lax
from jax.experimental import pallas as pl
from jax.experimental.pallas import tpu as pltpu
from jax.sharding import PartitionSpec as P

L = 101
ROUNDS = 2

eps_power = 1e-06
half_band = 2
tile_rows = 8
LANES = 128
K8 = 8
K16 = 16
K4 = 4
MIB = 2**20


def shortened(value):

    def short(part):
        return part.astype(jnp.bfloat16) if part.dtype == jnp.float32 else part

    return jax.tree.map(short, value)


def partner(value, axis, distance):
    mask = 2**distance
    pairs = [(source, source ^ mask) for source in range(lax.axis_size(axis))]
    return lax.ppermute(value, axis, pairs)


def band_mean(power, windows):
    nbins = power.shape[1]
    padded = jnp.pad(power, ((0, 0), (half_band, half_band)))
    ones = jnp.pad(jnp.ones((nbins,), jnp.float32), (half_band, half_band))
    total = padded[:, 0:nbins]
    count = ones[0:nbins]
    for offset in range(1, 2 * half_band + 1):
        total = total + padded[:, offset : offset + nbins]
        count = count + ones[offset : offset + nbins]
    return total / (count * windows)


def power_of(parts):
    value_array = parts.astype(jnp.float32)
    return jnp.sum(value_array * value_array, axis=(0, 1))


def whiten(parts, power, windows):
    scale = lax.rsqrt(band_mean(power, windows) + eps_power)
    return (parts.astype(jnp.float32) * scale).astype(jnp.bfloat16)


def lag_table(nbins, nlags, windows):
    samples = 2 * (nbins - 1)
    freq = jnp.arange(nbins, dtype=jnp.int32)
    lags = jnp.arange(nlags, dtype=jnp.int32) - (nlags - 1) // 2
    phase_index = freq[:, None] * lags[None, :] % samples
    angle = 2.0 * math.pi / samples * phase_index.astype(jnp.float32)
    weight = jnp.where((freq == 0) | (freq == nbins - 1), 1.0, 2.0).astype(jnp.float32)
    norm = 1.0 / math.sqrt(windows * samples)
    cos_part = weight[:, None] * jnp.cos(angle) * norm
    sin_part = -weight[:, None] * jnp.sin(angle) * norm
    return jnp.concatenate([cos_part, sin_part], axis=0)


def correlate(sources, receivers, table):
    left = jnp.concatenate([sources[0], sources[1]], axis=0)
    turned = jnp.concatenate([sources[1], -sources[0]], axis=0)
    right = jnp.concatenate([receivers[0], receivers[1]], axis=0)
    count = left.shape[1] // tile_rows

    def one_tile(index):
        start = index * tile_rows
        part_left = lax.dynamic_slice_in_dim(left, start, tile_rows, 1)
        part_turned = lax.dynamic_slice_in_dim(turned, start, tile_rows, 1)
        real = jnp.einsum("wak,wbk->kab", part_left, right, preferred_element_type=jnp.float32)
        imag = jnp.einsum("wak,wbk->kab", part_turned, right, preferred_element_type=jnp.float32)
        stacked = jnp.concatenate([real, imag], axis=0)
        return jnp.einsum("kab,kl->alb", stacked, table, precision=lax.Precision.HIGHEST)

    result = lax.map(one_tile, jnp.arange(count, dtype=jnp.int32))
    return result.reshape(count * tile_rows, table.shape[1], right.shape[1]).astype(jnp.bfloat16)


def make_walker(mask_bits, depth):

    def walker(moving):
        for bit in range(depth):
            if mask_bits >> bit & 1:
                moving = jax.tree.map(
                    lambda part, own: part.astype(own.dtype),
                    partner(shortened(moving), "blk", bit),
                    moving,
                )
        return moving

    return walker


def walking_body(spectra, channel_slot, partners):
    n_blk = lax.axis_size("blk")
    n_win = lax.axis_size("win")
    chans = spectra.shape[2]
    nbins = spectra.shape[3]
    per_peer = chans // n_blk
    here = lax.axis_index("blk")
    target = channel_slot // chans * per_peer + channel_slot % chans - here * per_peer
    selector = (jnp.arange(chans, dtype=jnp.int32)[:, None] == target[None, :]).astype(jnp.bfloat16)
    ordered = jnp.einsum(
        "pc,rwcf->rwpf", selector, spectra, preferred_element_type=jnp.float32
    ).astype(jnp.bfloat16)
    blocked = lax.all_to_all(ordered, "blk", split_axis=2, concat_axis=2, tiled=True)
    windows = spectra.shape[1] * n_win
    power = lax.psum(power_of(blocked), "win")
    outgoing = whiten(blocked, power, windows)
    own_all = lax.all_gather(outgoing, "win", axis=1, tiled=True)
    share = chans // n_win
    sources = lax.dynamic_slice_in_dim(own_all, lax.axis_index("win") * share, share, 2)
    table = lag_table(nbins, L, windows)
    masks = jnp.bitwise_xor(partners[:, here], here)
    bits = n_blk.bit_length() - 1
    results = []
    walkers = [make_walker(mask_bits, bits) for mask_bits in range(1, n_blk)]
    for round_index in range(ROUNDS):
        moving = lax.switch(masks[round_index] - 1, walkers, outgoing)
        partner_all = jax.tree.map(
            lambda part, own: part.astype(own.dtype),
            lax.all_gather(shortened(moving), "win", axis=1, tiled=True),
            moving,
        )
        results.append(correlate(sources, partner_all, table))
    return jnp.stack(results, axis=0)


def iota(shape, dim):
    return lax.broadcasted_iota(jnp.int32, shape, dim)


def bins_of(nbins):
    return -(-nbins // K16)


def lag_matrix(nbins):
    samples = 2 * (nbins - 1)
    groups = 2 * bins_of(nbins)
    rows = -(-L // K8) * K8
    freq = np.arange(nbins)
    lags = np.arange(L) - (L - 1) // 2
    angle = 2.0 * np.pi / samples * (freq[:, None] * lags[None, :] % samples)
    weight = np.where((freq == 0) | (freq == nbins - 1), 1.0, 2.0)[:, None]
    full = np.zeros((rows, 2, groups * K8))
    full[:L, 0, :nbins] = (weight * np.cos(angle)).T
    full[:L, 1, :nbins] = -(weight * np.sin(angle)).T
    full = full.reshape(rows, 2, 2 * groups, K4).transpose(0, 2, 1, 3).reshape(rows, groups * 2 * K8)
    return full.astype(jnp.bfloat16)


def top(shape):
    return iota(shape, 0) % K8 < K4


def moved_by(value, rows):
    return pltpu.roll(value, rows % value.shape[0], 0)


def low_rows(first, second):
    return jnp.where(top(first.shape), first, moved_by(second, K4))


def high_rows(first, second):
    return jnp.where(top(first.shape), moved_by(first, -K4), second)


def tiles_of(first, second, third):
    return low_rows(first, second), third, high_rows(first, second)


def bins_from(tiles):
    low, both, high = tiles
    rest = jnp.where(top(low.shape), low + moved_by(low, -K4), high + moved_by(high, K4))
    return both + rest


def pack_kernel(layout, nbins, here_ref, part_ref, slot_ref, x_ref, *rest):
    outs, (wide_ref, blocks_ref) = rest[: len(layout)], rest[len(layout) :]
    n_blk, n_grp, n_row, lanes = blocks_ref.shape
    per_peer = lanes // 4
    chans = slot_ref.shape[1]
    here = here_ref[0]
    slot = slot_ref[...]
    target = slot // chans * per_peer + slot % chans - here * per_peer
    shape = (n_blk * lanes, chans)
    row = iota(shape, 0)
    pick = jnp.where(target == row // lanes * per_peer + row % per_peer, 1.0, 0.0).astype(jnp.bfloat16)
    rows = math.prod(x_ref.shape[:-1])
    wide = lax.dot_general(x_ref[...].reshape(rows, chans), pick, (((1,), (1,)), ((), ())), preferred_element_type=jnp.float32)
    for block in range(n_blk):
        wide_ref[block, pl.ds(0, rows), :] = wide[:, block * lanes : (block + 1) * lanes]
    bins = n_grp * K16
    lane_group = iota((bins, lanes), 1) // per_peer
    inside = iota((bins, lanes), 0) < nbins
    for block in range(n_blk):
        values = []
        for pair in range(3):
            value = jnp.zeros((bins, lanes), jnp.float32)
            for g in range(4):
                start = (2 * pair + g % 2) * 2 * nbins + g // 2
                value = jnp.where(lane_group == g, wide_ref[block, pl.ds(start, bins, stride=2), :], value)
            values.append(jnp.where(inside, value, 0.0))
        tiles = [tile.reshape(n_grp, 2, 1, K8, lanes) for tile in tiles_of(*values)]
        blocks_ref[block] = jnp.concatenate(tiles, axis=2).reshape(n_grp, n_row, lanes).astype(jnp.bfloat16)
    masks = [part_ref[r, here] ^ here for r in range(ROUNDS)]
    masks.append(masks[0] ^ masks[1])
    for out, message in zip(outs, layout):
        for place, (step, name) in enumerate(message):
            mask = 0 if name is None else masks[name]
            out[place] = blocks_ref[here ^ step ^ mask]


def scale_of(power_ref, nbins, windows):
    rows = power_ref.shape[0] - 2 * K8
    total = power_ref[pl.ds(K8 - half_band, rows), :]
    for offset in range(1, 2 * half_band + 1):
        total = total + power_ref[pl.ds(K8 - half_band + offset, rows), :]
    bin_ = iota(total.shape, 0)
    count = jnp.minimum(bin_ + half_band, nbins - 1) - jnp.maximum(bin_ - half_band, 0) + 1
    count = jnp.maximum(count, 1).astype(jnp.float32)
    return lax.rsqrt(total / (count * windows) + eps_power)


def source_kernel(nbins, windows, *refs):
    src, (out_ref, power_ref, scale_ref, copies_ref) = refs[:4], refs[4:]
    n_grp, n_row, lanes = src[0].shape[1:]
    share = lanes // 4
    step = pl.program_id(0)

    @pl.when(step == 0)
    def _():
        totals = [jnp.zeros((n_grp, 2, K8, lanes), jnp.float32) for _ in range(3)]
        for ref in src:
            value = ref[0].astype(jnp.float32).reshape(n_grp, 2, 3, K8, lanes)
            totals = [total + value[:, :, i] * value[:, :, i] for i, total in enumerate(totals)]
        total = bins_from([total.reshape(n_grp * K16, lanes) for total in totals])
        total = total + pltpu.roll(total, 2 * share, 1)
        total = total + pltpu.roll(total, share, 1)
        power_ref[...] = jnp.zeros(power_ref.shape, jnp.float32)
        power_ref[pl.ds(K8, n_grp * K16), :] = total
        scale = scale_of(power_ref, nbins, windows)
        scales = [low_rows(scale, scale), scale, high_rows(scale, scale)]
        scales = [value.reshape(n_grp, 2, 1, K8, lanes) for value in scales]
        scale_ref[...] = jnp.concatenate(scales, axis=2).reshape(scale_ref.shape)
        row, col = iota(copies_ref.shape, 0), iota(copies_ref.shape, 1)
        same = (col % share == row // K8) & (col // share == row // K4 % 2)
        copies_ref[...] = jnp.where(same, 1.0, 0.0).astype(jnp.bfloat16)

    scale = scale_ref[step]
    white = [(ref[0, step].astype(jnp.float32) * scale).astype(jnp.bfloat16).astype(jnp.float32) for ref in src]
    lane = iota((share, lanes), 1)
    shape = (copies_ref.shape[0], 2 * lanes)
    keep = iota(shape, 0) % K4 == iota(shape, 1) % K4
    for half in range(2):
        tiles = [[value[(3 * half + i) * K8 : (3 * half + i + 1) * K8] for value in white] for i in range(3)]
        third = tiles[1]
        rows = tiles[0] + [low_rows(third[0], third[1]), low_rows(third[2], third[3])]
        rows = rows + tiles[2] + [high_rows(third[0], third[1]), high_rows(third[2], third[3])]
        width = len(rows) * K4
        rows = rows + [jnp.zeros((lanes - len(rows) * K8, lanes), jnp.float32)]
        turned = jnp.concatenate(rows, axis=0).T
        by_group = [turned[g * share : (g + 1) * share] for g in range(4)]
        crossed = [by_group[2], by_group[3], -by_group[0], -by_group[1]]
        for group in range(2):
            lines = []
            for values in (by_group, crossed):
                for start, size in ((0, 8 * K4), (8 * K4, 4 * K4)):
                    line = jnp.zeros((share, lanes), jnp.float32)
                    for g in range(4):
                        shift = (g * size - group * width - start) % lanes
                        moved = pltpu.roll(values[g], shift, 1) if shift else values[g]
                        line = jnp.where(lane // size == g, moved, line)
                    lines.append(line)
            lines = jnp.concatenate(
                [jnp.concatenate(lines[:2], axis=1), jnp.concatenate(lines[2:], axis=1)], axis=0
            ).astype(jnp.bfloat16)
            spread = jnp.dot(copies_ref[...], lines, preferred_element_type=jnp.float32)
            spread = jnp.where(keep, spread, 0.0).astype(jnp.bfloat16)
            out_ref[2 * half + group] = spread[:, : out_ref.shape[2]]


def take_pieces(pieces, places, phase, here, right_ref, power_ref, scale_ref, nbins, windows):
    n_grp, n_row, lanes = pieces[0].shape[1:]
    share = lanes // 4
    shape = (4 * lanes, 4 * lanes)
    row, col = iota(shape, 0), iota(shape, 1)
    kind = row // lanes
    half = (here >> 1) ^ phase ^ (kind >> 1)
    odd = (here ^ kind) & 1
    spot = row % lanes // share * lanes + (2 * half + odd) * share + row % share
    order = jnp.where(col == spot, 1.0, 0.0).astype(jnp.bfloat16)
    flat, tall = (n_grp * K16, lanes), (n_grp, 2, K8, lanes)
    totals = [jnp.zeros(tall, jnp.float32) for _ in range(3)]
    before = [None] * 4
    for e in range(4):
        parts = [pieces[operand][index].reshape(n_grp * n_row, lanes) for operand, index in places[e]]
        moved = jnp.dot(jnp.concatenate(parts, axis=1), order, preferred_element_type=jnp.float32)
        moved = moved.reshape(n_grp, 2, 3, K8, 4 * lanes)
        for g in range(4):
            low, both, high = values = [moved[:, :, i, :, g * lanes : (g + 1) * lanes] for i in range(3)]
            totals = [total + value * value for total, value in zip(totals, values)]
            right_ref[:, :, 0, g * 4 + e] = low
            right_ref[:, :, 1, g * 4 + e] = high
            both = both.reshape(flat)
            if e % 2:
                spot = 16 + g * 2 + e // 2
                right_ref[:, :, 0, spot] = low_rows(before[g], both).reshape(tall)
                right_ref[:, :, 1, spot] = high_rows(before[g], both).reshape(tall)
            before[g] = both
    power_ref[...] = jnp.zeros(power_ref.shape, jnp.float32)
    power_ref[pl.ds(K8, n_grp * K16), :] = bins_from([total.reshape(flat) for total in totals])
    scale = scale_of(power_ref, nbins, windows)
    scale_ref[:, :, 0] = low_rows(scale, scale).reshape(tall)
    scale_ref[:, :, 1] = high_rows(scale, scale).reshape(tall)


def whitened(right_ref, scale_ref, index, half, group):
    white = (right_ref[index, half, group] * scale_ref[index, half, group]).astype(jnp.bfloat16)
    return white.reshape(-1, white.shape[-1])


def receive_kernel(places, nbins, windows, here_ref, *rest):
    pieces, (out_ref, right_ref, power_ref, scale_ref) = rest[:-4], rest[-4:]
    take_pieces(pieces, places, 0, here_ref[0], right_ref, power_ref, scale_ref, nbins, windows)

    def one_group(index, carry):
        for half in range(2):
            for group in range(2):
                out_ref[4 * index + 2 * half + group] = whitened(right_ref, scale_ref, index, half, group)
        return carry

    lax.fori_loop(0, right_ref.shape[0], one_group, 0)


def correlate_kernel(places, nbins, windows, here_ref, left_hbm, early_hbm, lag_ref, *rest):
    pieces, rest = rest[:-9], rest[-9:]
    out_ref, left_ref, early_ref, right_ref, cross_ref, lagged_ref, power_ref, scale_ref, sems = rest
    copies = [
        pltpu.make_async_copy(left_hbm, left_ref, sems.at[0]),
        pltpu.make_async_copy(early_hbm, early_ref, sems.at[1]),
    ]
    for copy in copies:
        copy.start()
    here = here_ref[0]
    take_pieces(pieces, places, 1, here, right_ref, power_ref, scale_ref, nbins, windows)
    for copy in copies:
        copy.wait()

    def one_group(index, carry):
        for half in range(2):
            crosses = []
            for group in range(2):
                spot = 4 * index + 2 * half + group
                both = jnp.concatenate([early_ref[spot], whitened(right_ref, scale_ref, index, half, group)], axis=1)
                cross = jnp.dot(left_ref[spot], both, preferred_element_type=jnp.float32)
                crosses.append(cross.reshape(-1, K8, cross.shape[-1]))
            place = pl.multiple_of((2 * index + half) * K16, K16)
            cross_ref[:, pl.ds(place, K16), :] = jnp.concatenate(crosses, axis=1).astype(jnp.bfloat16)
        return carry

    lax.fori_loop(0, right_ref.shape[0], one_group, 0)
    norm = 1.0 / math.sqrt(windows * 2 * (nbins - 1))
    share, lanes = cross_ref.shape[0], pieces[0].shape[-1]
    first = iota((lag_ref.shape[0], lanes), 1) // (2 * share) == here >> 1

    def one_source(index, carry):
        lagged = jnp.dot(lag_ref[...], cross_ref[index], preferred_element_type=jnp.float32) * norm
        early, late = lagged[:, :lanes], lagged[:, lanes:]
        rounds = [jnp.where(first, early, late), pltpu.roll(jnp.where(first, late, early), lanes // 2, 1)]
        for r in range(ROUNDS):
            lagged_ref[r, pl.ds(index, lagged.shape[0], stride=share), :] = rounds[r]
        return carry

    lax.fori_loop(0, share, one_source, 0, unroll=4)
    for r in range(ROUNDS):
        out_ref[r] = lagged_ref[r, pl.ds(0, L * share), :].astype(jnp.bfloat16).reshape(L, share, lanes)


def swap(value, axis, mask):
    return lax.ppermute(value, axis, [(i, i ^ mask) for i in range(lax.axis_size(axis))])


def call(kernel, outs, operands, scratch, name, specs=None, vmem_mib=40, **grid):
    return pl.pallas_call(
        kernel,
        cost_estimate=pl.CostEstimate(flops=0, bytes_accessed=MIB, transcendentals=0),
        out_shape=outs,
        in_specs=specs,
        scratch_shapes=scratch,
        compiler_params=pltpu.CompilerParams(vmem_limit_bytes=vmem_mib * MIB),
        name=name,
        **grid,
    )(*operands)


def after(value, *earlier):
    return lax.optimization_barrier((value, *earlier))[0]


def make_branch(case):
    one, other = (case, 1 - case) if case < 2 else (None, None)

    def branch(spectra, channel_slot, partners, here):
        chans, nbins = spectra.shape[2:]
        windows = spectra.shape[1] * lax.axis_size("win")
        n_grp = bins_of(nbins)
        share = chans // 4
        piece = (n_grp, 3 * K16, chans)
        win = lax.axis_index("win")
        if case < 2:
            layout = [[(2, one), (2, None)], [(2, 2), (2, other)]]
        else:
            layout = [[(2, None), (3, None)], [(2, 0), (2, 1)]]
        layout += [[(1, 0), (1, 1), (1, None)], [(0, 0), (0, 1)], [(0, None)]]
        vmem, smem = pl.BlockSpec(memory_space=pltpu.VMEM), pl.BlockSpec(memory_space=pltpu.SMEM)
        far_a, far_b, near, own, own_src = call(
            lambda *refs: pack_kernel(layout, nbins, *refs),
            [jax.ShapeDtypeStruct((len(m),) + piece, jnp.bfloat16) for m in layout],
            (here, partners, channel_slot.reshape(1, chans), spectra.transpose(1, 3, 0, 2)),
            [
                pltpu.VMEM((4, spectra.shape[1] * 2 * nbins + 4 * K16, chans), jnp.float32),
                pltpu.VMEM((4,) + piece, jnp.bfloat16),
            ],
            "pack",
            [smem, smem, vmem, vmem],
        )
        z = here[0]
        mine = (z >> 1) == (win >> 1)
        got_1 = swap(near, "blk", 1)
        got_a = swap(far_a, "blk", 2)
        over_0 = swap(own, "win", 2)
        over_1 = swap(after(got_1[:2], over_0), "win", 2)
        got_b = swap(after(far_b, got_a), "blk", 2)
        core_2b = swap(got_b, "win", 1)
        if case < 2:
            got_3a = swap(got_a, "blk", 1)
            over_2a = swap(got_a[:1], "win", 2)
            got_3b = swap(after(got_b[:1], core_2b), "blk", 1)
            src = [own_src, got_1[2:], got_a[1:], after(got_3a[:1], over_1, over_2a)]
        else:
            got_3a = swap(got_a[1:], "blk", 1)
            got_3b = swap(after(got_b, core_2b), "blk", 1)
            src = [own_src, got_1[2:], got_a[:1], after(got_3a, over_1)]
        high = [jnp.where(mine, src[d + 2], src[d]) for d in range(2)]
        across = swap(jnp.concatenate(high, axis=0), "win", 2)
        low = [jnp.where(mine, src[d], src[d + 2]) for d in range(2)]
        if case < 2:
            over_2b = swap(got_b[1:], "win", 2)
            over_3a = swap(got_3a[1:], "win", 2)
            over_3b = None
            arrays = {
                "2a": [got_a, over_2a],
                "3a": [got_3a, over_3a],
                "2b": [got_b, over_2b],
                "3b": [got_3b, over_3b],
            }
            held = {(other, 2): ("2b", (1, 0)), (one, 2): ("2a", (0, 0))}
            held |= {(other, 3): ("3b", (0, 0)), (one, 3): ("3a", (1, 0))}
        else:
            over_2b = swap(got_b, "win", 2)
            over_3b = None
            arrays = {"2b": [got_b, over_2b], "3b": [got_3b, over_3b]}
            held = {(r, 2): ("2b", (r, r)) for r in range(2)} | {(r, 3): ("3b", (1 - r, 1 - r)) for r in range(2)}
        arrays |= {0: [own, over_0], 1: [got_1, over_1]}
        held |= {(r, d): (d, (r, r)) for r in range(2) for d in range(2)}
        def doubled(name, last=()):
            held_here, over = arrays[name]
            core_here = core_2b if name == "2b" else swap(held_here, "win", 1)
            arrays[name] = [held_here, core_here, over, swap(after(over, *last) if last else over, "win", 1)]

        def places_of(phase):
            names = list(dict.fromkeys(held[r, d][0] for r in range(ROUNDS) for d in (2 * phase, 2 * phase + 1)))
            places = [[] for _ in range(4)]
            for r in range(ROUNDS):
                for d in (2 * phase, 2 * phase + 1):
                    name, (whole, part) = held[r, d]
                    for e in range(4):
                        size = arrays[name][e].shape[0]
                        index = whole if size == arrays[name][0].shape[0] else part
                        places[e].append((4 * names.index(name) + e, index))
            return places, [array for name in names for array in arrays[name]]

        for name in (0, 1):
            doubled(name)
        lag = jnp.asarray(lag_matrix(nbins))
        taken = [
            pltpu.VMEM((n_grp, 2, 2, 24, K8, chans), jnp.float32),
            pltpu.VMEM((n_grp * K16 + 2 * K8, chans), jnp.float32),
            pltpu.VMEM((n_grp, 2, 2, K8, chans), jnp.float32),
        ]
        early_places, early_pieces = places_of(0)
        early = call(
            lambda *refs: receive_kernel(early_places, nbins, windows, *refs),
            jax.ShapeDtypeStruct((4 * n_grp, 24 * K8, chans), jnp.bfloat16),
            (here, *early_pieces),
            taken,
            "receivers",
            [smem] + [vmem] * len(early_pieces),
        )
        over_3b = swap(got_3b, "win", 2)
        across = after(across, got_3b, early)
        odd = ((win ^ z) & 1) == 1
        first, second = low, [across[0:1], across[1:2]]
        sources = []
        for two in (first, second):
            sources.append(jnp.where(odd, two[1], two[0]))
            sources.append(swap(jnp.where(odd, two[0], two[1]), "win", 1))
        left = call(
            lambda *refs: source_kernel(nbins, windows, *refs),
            jax.ShapeDtypeStruct((4 * n_grp, share * K8, 3 * chans // 2), jnp.bfloat16),
            sources,
            [
                pltpu.VMEM((n_grp * K16 + 2 * K8, chans), jnp.float32),
                pltpu.VMEM((n_grp, 3 * K16, chans), jnp.float32),
                pltpu.VMEM((share * K8, 2 * share), jnp.bfloat16),
            ],
            "sources",
            [vmem] * 4,
            grid=(n_grp,),
            out_specs=pl.BlockSpec((4, share * K8, 3 * chans // 2), lambda i: (i, 0, 0)),
        )
        arrays["3b"] = [got_3b, over_3b]
        for name in list(arrays):
            if name not in (0, 1):
                doubled(name, [left] if name == "3b" else [])
        late_places, late_pieces = places_of(1)
        hbm = pl.BlockSpec(memory_space=pl.ANY)
        by_lag = call(
            lambda *refs: correlate_kernel(late_places, nbins, windows, *refs),
            jax.ShapeDtypeStruct((ROUNDS, L, share, chans), jnp.bfloat16),
            (here, left, early, lag, *late_pieces),
            [
                pltpu.VMEM(left.shape, jnp.bfloat16),
                pltpu.VMEM(early.shape, jnp.bfloat16),
                taken[0],
                pltpu.VMEM((share, n_grp * 4 * K8, ROUNDS * chans), jnp.bfloat16),
                pltpu.VMEM((ROUNDS, lag.shape[0] * share, chans), jnp.float32),
                *taken[1:],
                pltpu.SemaphoreType.DMA((2,)),
            ],
            "correlate",
            [smem, hbm, hbm] + [vmem] * (1 + len(late_pieces)),
        )
        return by_lag.transpose(0, 2, 1, 3)

    return branch


def gathering_body(spectra, channel_slot, partners):
    here = lax.axis_index("blk")
    masks = partners[:, 0]
    case = jnp.where(masks[0] == 1, 0, jnp.where(masks[1] == 1, 1, 2))
    branches = [make_branch(i) for i in range(3)]
    return lax.switch(case, branches, spectra, channel_slot, partners, here.reshape(1))


def solution(mesh):
    in_specs = (P(None, "win", ("groups", "blk"), None), P(("groups", "blk")), P())
    out_specs = P(None, ("groups", "blk", "win"), None, None)

    def body(spectra, channel_slot, partners):
        small = all((mesh.shape[axis] - 1).bit_length() == 2 for axis in ("blk", "win"))
        small = small and spectra.shape[2] == LANES and spectra.shape[1] // 2 == 3 and spectra.shape[3] <= 2 * LANES
        return (gathering_body if small else walking_body)(spectra, channel_slot, partners)

    return jax.shard_map(body, mesh=mesh, in_specs=in_specs, out_specs=out_specs, check_vma=False)
```

```python
import math

import jax
import jax.numpy as jnp
import numpy as np
from jax import lax
from jax.experimental import pallas as pl
from jax.experimental.pallas import tpu as pltpu
from jax.sharding import PartitionSpec as P

L = 101
ROUNDS = 2

eps_power = 1e-06
half_band = 2
tile_rows = 8
LANES = 128
K8 = 8
K16 = 16
K4 = 4
MIB = 2**20


def shortened(value):

    def short(part):
        return part.astype(jnp.bfloat16) if part.dtype == jnp.float32 else part

    return jax.tree.map(short, value)


def partner(value, axis, distance):
    mask = 2**distance
    pairs = [(source, source ^ mask) for source in range(lax.axis_size(axis))]
    return lax.ppermute(value, axis, pairs)


def band_mean(power, windows):
    nbins = power.shape[1]
    padded = jnp.pad(power, ((0, 0), (half_band, half_band)))
    ones = jnp.pad(jnp.ones((nbins,), jnp.float32), (half_band, half_band))
    total = padded[:, 0:nbins]
    count = ones[0:nbins]
    for offset in range(1, 2 * half_band + 1):
        total = total + padded[:, offset : offset + nbins]
        count = count + ones[offset : offset + nbins]
    return total / (count * windows)


def power_of(parts):
    value_array = parts.astype(jnp.float32)
    return jnp.sum(value_array * value_array, axis=(0, 1))


def whiten(parts, power, windows):
    scale = lax.rsqrt(band_mean(power, windows) + eps_power)
    return (parts.astype(jnp.float32) * scale).astype(jnp.bfloat16)


def lag_table(nbins, nlags, windows):
    samples = 2 * (nbins - 1)
    freq = jnp.arange(nbins, dtype=jnp.int32)
    lags = jnp.arange(nlags, dtype=jnp.int32) - (nlags - 1) // 2
    phase_index = freq[:, None] * lags[None, :] % samples
    angle = 2.0 * math.pi / samples * phase_index.astype(jnp.float32)
    weight = jnp.where((freq == 0) | (freq == nbins - 1), 1.0, 2.0).astype(jnp.float32)
    norm = 1.0 / math.sqrt(windows * samples)
    cos_part = weight[:, None] * jnp.cos(angle) * norm
    sin_part = -weight[:, None] * jnp.sin(angle) * norm
    return jnp.concatenate([cos_part, sin_part], axis=0)


def correlate(sources, receivers, table):
    left = jnp.concatenate([sources[0], sources[1]], axis=0)
    turned = jnp.concatenate([sources[1], -sources[0]], axis=0)
    right = jnp.concatenate([receivers[0], receivers[1]], axis=0)
    count = left.shape[1] // tile_rows

    def one_tile(index):
        start = index * tile_rows
        part_left = lax.dynamic_slice_in_dim(left, start, tile_rows, 1)
        part_turned = lax.dynamic_slice_in_dim(turned, start, tile_rows, 1)
        real = jnp.einsum("wak,wbk->kab", part_left, right, preferred_element_type=jnp.float32)
        imag = jnp.einsum("wak,wbk->kab", part_turned, right, preferred_element_type=jnp.float32)
        stacked = jnp.concatenate([real, imag], axis=0)
        return jnp.einsum("kab,kl->alb", stacked, table, precision=lax.Precision.HIGHEST)

    result = lax.map(one_tile, jnp.arange(count, dtype=jnp.int32))
    return result.reshape(count * tile_rows, table.shape[1], right.shape[1]).astype(jnp.bfloat16)


def make_walker(mask_bits, depth):

    def walker(moving):
        for bit in range(depth):
            if mask_bits >> bit & 1:
                moving = jax.tree.map(
                    lambda part, own: part.astype(own.dtype),
                    partner(shortened(moving), "blk", bit),
                    moving,
                )
        return moving

    return walker


def walking_body(spectra, channel_slot, partners):
    n_blk = lax.axis_size("blk")
    n_win = lax.axis_size("win")
    chans = spectra.shape[2]
    nbins = spectra.shape[3]
    per_peer = chans // n_blk
    here = lax.axis_index("blk")
    target = channel_slot // chans * per_peer + channel_slot % chans - here * per_peer
    selector = (jnp.arange(chans, dtype=jnp.int32)[:, None] == target[None, :]).astype(jnp.bfloat16)
    ordered = jnp.einsum(
        "pc,rwcf->rwpf", selector, spectra, preferred_element_type=jnp.float32
    ).astype(jnp.bfloat16)
    blocked = lax.all_to_all(ordered, "blk", split_axis=2, concat_axis=2, tiled=True)
    windows = spectra.shape[1] * n_win
    power = lax.psum(power_of(blocked), "win")
    outgoing = whiten(blocked, power, windows)
    own_all = lax.all_gather(outgoing, "win", axis=1, tiled=True)
    share = chans // n_win
    sources = lax.dynamic_slice_in_dim(own_all, lax.axis_index("win") * share, share, 2)
    table = lag_table(nbins, L, windows)
    masks = jnp.bitwise_xor(partners[:, here], here)
    bits = n_blk.bit_length() - 1
    results = []
    walkers = [make_walker(mask_bits, bits) for mask_bits in range(1, n_blk)]
    for round_index in range(ROUNDS):
        moving = lax.switch(masks[round_index] - 1, walkers, outgoing)
        partner_all = jax.tree.map(
            lambda part, own: part.astype(own.dtype),
            lax.all_gather(shortened(moving), "win", axis=1, tiled=True),
            moving,
        )
        results.append(correlate(sources, partner_all, table))
    return jnp.stack(results, axis=0)


def iota(shape, dim):
    return lax.broadcasted_iota(jnp.int32, shape, dim)


def bins_of(nbins):
    return -(-nbins // K16)


def lag_matrix(nbins):
    samples = 2 * (nbins - 1)
    groups = 2 * bins_of(nbins)
    rows = -(-L // K8) * K8
    freq = np.arange(nbins)
    lags = np.arange(L) - (L - 1) // 2
    angle = 2.0 * np.pi / samples * (freq[:, None] * lags[None, :] % samples)
    weight = np.where((freq == 0) | (freq == nbins - 1), 1.0, 2.0)[:, None]
    full = np.zeros((rows, 2, groups * K8))
    full[:L, 0, :nbins] = (weight * np.cos(angle)).T
    full[:L, 1, :nbins] = -(weight * np.sin(angle)).T
    full = full.reshape(rows, 2, 2 * groups, K4).transpose(0, 2, 1, 3).reshape(rows, groups * 2 * K8)
    return full.astype(jnp.bfloat16)


def top(shape):
    return iota(shape, 0) % K8 < K4


def moved_by(value, rows):
    return pltpu.roll(value, rows % value.shape[0], 0)


def low_rows(first, second):
    return jnp.where(top(first.shape), first, moved_by(second, K4))


def high_rows(first, second):
    return jnp.where(top(first.shape), moved_by(first, -K4), second)


def tiles_of(first, second, third):
    return low_rows(first, second), third, high_rows(first, second)


def bins_from(tiles):
    low, both, high = tiles
    rest = jnp.where(top(low.shape), low + moved_by(low, -K4), high + moved_by(high, K4))
    return both + rest


def pack_kernel(layout, nbins, here_ref, part_ref, slot_ref, x_ref, *rest):
    outs, (wide_ref, blocks_ref) = rest[: len(layout)], rest[len(layout) :]
    n_blk, n_grp, n_row, lanes = blocks_ref.shape
    per_peer = lanes // 4
    chans = slot_ref.shape[1]
    here = here_ref[0]
    slot = slot_ref[...]
    target = slot // chans * per_peer + slot % chans - here * per_peer
    shape = (n_blk * lanes, chans)
    row = iota(shape, 0)
    pick = jnp.where(target == row // lanes * per_peer + row % per_peer, 1.0, 0.0).astype(jnp.bfloat16)
    rows = math.prod(x_ref.shape[:-1])
    wide = lax.dot_general(x_ref[...].reshape(rows, chans), pick, (((1,), (1,)), ((), ())), preferred_element_type=jnp.float32)
    for block in range(n_blk):
        wide_ref[block, pl.ds(0, rows), :] = wide[:, block * lanes : (block + 1) * lanes]
    bins = n_grp * K16
    lane_group = iota((bins, lanes), 1) // per_peer
    inside = iota((bins, lanes), 0) < nbins
    for block in range(n_blk):
        values = []
        for pair in range(3):
            value = jnp.zeros((bins, lanes), jnp.float32)
            for g in range(4):
                start = (2 * pair + g % 2) * 2 * nbins + g // 2
                value = jnp.where(lane_group == g, wide_ref[block, pl.ds(start, bins, stride=2), :], value)
            values.append(jnp.where(inside, value, 0.0))
        tiles = [tile.reshape(n_grp, 2, 1, K8, lanes) for tile in tiles_of(*values)]
        blocks_ref[block] = jnp.concatenate(tiles, axis=2).reshape(n_grp, n_row, lanes).astype(jnp.bfloat16)
    masks = [part_ref[r, here] ^ here for r in range(ROUNDS)]
    masks.append(masks[0] ^ masks[1])
    for out, message in zip(outs, layout):
        for place, (step, name) in enumerate(message):
            mask = 0 if name is None else masks[name]
            out[place] = blocks_ref[here ^ step ^ mask]


def scale_of(power_ref, nbins, windows):
    rows = power_ref.shape[0] - 2 * K8
    total = power_ref[pl.ds(K8 - half_band, rows), :]
    for offset in range(1, 2 * half_band + 1):
        total = total + power_ref[pl.ds(K8 - half_band + offset, rows), :]
    bin_ = iota(total.shape, 0)
    count = jnp.minimum(bin_ + half_band, nbins - 1) - jnp.maximum(bin_ - half_band, 0) + 1
    count = jnp.maximum(count, 1).astype(jnp.float32)
    return lax.rsqrt(total / (count * windows) + eps_power)


def source_kernel(nbins, windows, *refs):
    src, (out_ref, power_ref, scale_ref, copies_ref) = refs[:4], refs[4:]
    n_grp, n_row, lanes = src[0].shape[1:]
    share = lanes // 4
    step = pl.program_id(0)

    @pl.when(step == 0)
    def _():
        totals = [jnp.zeros((n_grp, 2, K8, lanes), jnp.float32) for _ in range(3)]
        for ref in src:
            value = ref[0].astype(jnp.float32).reshape(n_grp, 2, 3, K8, lanes)
            totals = [total + value[:, :, i] * value[:, :, i] for i, total in enumerate(totals)]
        total = bins_from([total.reshape(n_grp * K16, lanes) for total in totals])
        total = total + pltpu.roll(total, 2 * share, 1)
        total = total + pltpu.roll(total, share, 1)
        power_ref[...] = jnp.zeros(power_ref.shape, jnp.float32)
        power_ref[pl.ds(K8, n_grp * K16), :] = total
        scale = scale_of(power_ref, nbins, windows)
        scales = [low_rows(scale, scale), scale, high_rows(scale, scale)]
        scales = [value.reshape(n_grp, 2, 1, K8, lanes) for value in scales]
        scale_ref[...] = jnp.concatenate(scales, axis=2).reshape(scale_ref.shape)
        row, col = iota(copies_ref.shape, 0), iota(copies_ref.shape, 1)
        same = (col % share == row // K8) & (col // share == row // K4 % 2)
        copies_ref[...] = jnp.where(same, 1.0, 0.0).astype(jnp.bfloat16)

    scale = scale_ref[step]
    white = [(ref[0, step].astype(jnp.float32) * scale).astype(jnp.bfloat16).astype(jnp.float32) for ref in src]
    lane = iota((share, lanes), 1)
    shape = (copies_ref.shape[0], 2 * lanes)
    keep = iota(shape, 0) % K4 == iota(shape, 1) % K4
    for half in range(2):
        tiles = [[value[(3 * half + i) * K8 : (3 * half + i + 1) * K8] for value in white] for i in range(3)]
        third = tiles[1]
        rows = tiles[0] + [low_rows(third[0], third[1]), low_rows(third[2], third[3])]
        rows = rows + tiles[2] + [high_rows(third[0], third[1]), high_rows(third[2], third[3])]
        width = len(rows) * K4
        rows = rows + [jnp.zeros((lanes - len(rows) * K8, lanes), jnp.float32)]
        turned = jnp.concatenate(rows, axis=0).T
        by_group = [turned[g * share : (g + 1) * share] for g in range(4)]
        crossed = [by_group[2], by_group[3], -by_group[0], -by_group[1]]
        for group in range(2):
            lines = []
            for values in (by_group, crossed):
                for start, size in ((0, 8 * K4), (8 * K4, 4 * K4)):
                    line = jnp.zeros((share, lanes), jnp.float32)
                    for g in range(4):
                        shift = (g * size - group * width - start) % lanes
                        moved = pltpu.roll(values[g], shift, 1) if shift else values[g]
                        line = jnp.where(lane // size == g, moved, line)
                    lines.append(line)
            lines = jnp.concatenate(
                [jnp.concatenate(lines[:2], axis=1), jnp.concatenate(lines[2:], axis=1)], axis=0
            ).astype(jnp.bfloat16)
            spread = jnp.dot(copies_ref[...], lines, preferred_element_type=jnp.float32)
            spread = jnp.where(keep, spread, 0.0).astype(jnp.bfloat16)
            out_ref[2 * half + group] = spread[:, : out_ref.shape[2]]


def take_pieces(pieces, places, phase, here, right_ref, power_ref, scale_ref, nbins, windows):
    n_grp, n_row, lanes = pieces[0].shape[1:]
    share = lanes // 4
    shape = (4 * lanes, 4 * lanes)
    row, col = iota(shape, 0), iota(shape, 1)
    kind = row // lanes
    half = (here >> 1) ^ phase ^ (kind >> 1)
    odd = (here ^ kind) & 1
    spot = row % lanes // share * lanes + (2 * half + odd) * share + row % share
    order = jnp.where(col == spot, 1.0, 0.0).astype(jnp.bfloat16)
    flat, tall = (n_grp * K16, lanes), (n_grp, 2, K8, lanes)
    totals = [jnp.zeros(tall, jnp.float32) for _ in range(3)]
    before = [None] * 4
    for e in range(4):
        parts = [pieces[operand][index].reshape(n_grp * n_row, lanes) for operand, index in places[e]]
        moved = jnp.dot(jnp.concatenate(parts, axis=1), order, preferred_element_type=jnp.float32)
        moved = moved.reshape(n_grp, 2, 3, K8, 4 * lanes)
        for g in range(4):
            low, both, high = values = [moved[:, :, i, :, g * lanes : (g + 1) * lanes] for i in range(3)]
            totals = [total + value * value for total, value in zip(totals, values)]
            right_ref[:, :, 0, g * 4 + e] = low
            right_ref[:, :, 1, g * 4 + e] = high
            both = both.reshape(flat)
            if e % 2:
                spot = 16 + g * 2 + e // 2
                right_ref[:, :, 0, spot] = low_rows(before[g], both).reshape(tall)
                right_ref[:, :, 1, spot] = high_rows(before[g], both).reshape(tall)
            before[g] = both
    power_ref[...] = jnp.zeros(power_ref.shape, jnp.float32)
    power_ref[pl.ds(K8, n_grp * K16), :] = bins_from([total.reshape(flat) for total in totals])
    scale = scale_of(power_ref, nbins, windows)
    scale_ref[:, :, 0] = low_rows(scale, scale).reshape(tall)
    scale_ref[:, :, 1] = high_rows(scale, scale).reshape(tall)


def whitened(right_ref, scale_ref, index, half, group):
    white = (right_ref[index, half, group] * scale_ref[index, half, group]).astype(jnp.bfloat16)
    return white.reshape(-1, white.shape[-1])


def receive_kernel(places, nbins, windows, here_ref, *rest):
    pieces, (out_ref, right_ref, power_ref, scale_ref) = rest[:-4], rest[-4:]
    take_pieces(pieces, places, 0, here_ref[0], right_ref, power_ref, scale_ref, nbins, windows)

    def one_group(index, carry):
        for half in range(2):
            for group in range(2):
                out_ref[4 * index + 2 * half + group] = whitened(right_ref, scale_ref, index, half, group)
        return carry

    lax.fori_loop(0, right_ref.shape[0], one_group, 0)


def correlate_kernel(places, nbins, windows, here_ref, left_hbm, early_hbm, lag_ref, *rest):
    pieces, rest = rest[:-9], rest[-9:]
    out_ref, left_ref, early_ref, right_ref, cross_ref, lagged_ref, power_ref, scale_ref, sems = rest
    copies = [
        pltpu.make_async_copy(left_hbm, left_ref, sems.at[0]),
        pltpu.make_async_copy(early_hbm, early_ref, sems.at[1]),
    ]
    for copy in copies:
        copy.start()
    here = here_ref[0]
    take_pieces(pieces, places, 1, here, right_ref, power_ref, scale_ref, nbins, windows)
    for copy in copies:
        copy.wait()

    def one_group(index, carry):
        for half in range(2):
            crosses = []
            for group in range(2):
                spot = 4 * index + 2 * half + group
                both = jnp.concatenate([early_ref[spot], whitened(right_ref, scale_ref, index, half, group)], axis=1)
                cross = jnp.dot(left_ref[spot], both, preferred_element_type=jnp.float32)
                crosses.append(cross.reshape(-1, K8, cross.shape[-1]))
            place = pl.multiple_of((2 * index + half) * K16, K16)
            cross_ref[:, pl.ds(place, K16), :] = jnp.concatenate(crosses, axis=1).astype(jnp.bfloat16)
        return carry

    lax.fori_loop(0, right_ref.shape[0], one_group, 0)
    norm = 1.0 / math.sqrt(windows * 2 * (nbins - 1))
    share, lanes = cross_ref.shape[0], pieces[0].shape[-1]
    first = iota((lag_ref.shape[0], lanes), 1) // (2 * share) == here >> 1

    def one_source(index, carry):
        lagged = jnp.dot(lag_ref[...], cross_ref[index], preferred_element_type=jnp.float32) * norm
        early, late = lagged[:, :lanes], lagged[:, lanes:]
        rounds = [jnp.where(first, early, late), pltpu.roll(jnp.where(first, late, early), lanes // 2, 1)]
        for r in range(ROUNDS):
            lagged_ref[r, pl.ds(index, lagged.shape[0], stride=share), :] = rounds[r]
        return carry

    lax.fori_loop(0, share, one_source, 0, unroll=4)
    for r in range(ROUNDS):
        out_ref[r] = lagged_ref[r, pl.ds(0, L * share), :].astype(jnp.bfloat16).reshape(L, share, lanes)


def swap(value, axis, mask):
    return lax.ppermute(value, axis, [(i, i ^ mask) for i in range(lax.axis_size(axis))])


def call(kernel, outs, operands, scratch, name, specs=None, vmem_mib=40, **grid):
    return pl.pallas_call(
        kernel,
        cost_estimate=pl.CostEstimate(flops=0, bytes_accessed=MIB, transcendentals=0),
        out_shape=outs,
        in_specs=specs,
        scratch_shapes=scratch,
        compiler_params=pltpu.CompilerParams(vmem_limit_bytes=vmem_mib * MIB),
        name=name,
        **grid,
    )(*operands)


def after(value, *earlier):
    return lax.optimization_barrier((value, *earlier))[0]


def make_branch(case):
    one, other = (case, 1 - case) if case < 2 else (None, None)

    def branch(spectra, channel_slot, partners, here):
        chans, nbins = spectra.shape[2:]
        windows = spectra.shape[1] * lax.axis_size("win")
        n_grp = bins_of(nbins)
        share = chans // 4
        piece = (n_grp, 3 * K16, chans)
        win = lax.axis_index("win")
        layout = [[(3, None), (2, None)], [(2, 2), (2, other)] if case < 2 else [(2, 0), (2, 1)]]
        layout += [[(1, 0), (1, 1), (1, None)], [(0, 0), (0, 1)], [(0, None)]]
        vmem, smem = pl.BlockSpec(memory_space=pltpu.VMEM), pl.BlockSpec(memory_space=pltpu.SMEM)
        far_a, far_b, near, own, own_src = call(
            lambda *refs: pack_kernel(layout, nbins, *refs),
            [jax.ShapeDtypeStruct((len(m),) + piece, jnp.bfloat16) for m in layout],
            (here, partners, channel_slot.reshape(1, chans), spectra.transpose(1, 3, 0, 2)),
            [
                pltpu.VMEM((4, spectra.shape[1] * 2 * nbins + 4 * K16, chans), jnp.float32),
                pltpu.VMEM((4,) + piece, jnp.bfloat16),
            ],
            "pack",
            [smem, smem, vmem, vmem],
        )
        z = here[0]
        mine = (z >> 1) == (win >> 1)
        got_1 = swap(near, "blk", 1)
        got_a = swap(far_a, "blk", 2)
        got_b = swap(after(far_b, got_a), "blk", 2)
        over_0 = swap(own, "win", 2)
        near_2, far_2, passed = got_1[:2], got_b, got_b
        if case < 2:
            far_2 = jnp.concatenate([got_a[:1], got_b[1:]], axis=0)
            passed = jnp.concatenate([got_a[1:], got_b[:1]], axis=0)
        over_1 = swap(after(near_2, over_0), "win", 2)
        got_src = swap(got_a[:1], "blk", 1)
        over_2 = swap(far_2, "win", 2)
        src = [own_src, got_1[2:], got_a[1:], after(got_src, over_1)]
        high = [jnp.where(mine, src[d + 2], src[d]) for d in range(2)]
        across = swap(jnp.concatenate(high, axis=0), "win", 2)
        low = [jnp.where(mine, src[d], src[d + 2]) for d in range(2)]
        got_3 = swap(after(passed, over_1, across), "blk", 1)
        odd = ((win ^ z) & 1) == 1
        first, second = low, [across[0:1], across[1:2]]
        sources = []
        for two in (first, second):
            sources.append(jnp.where(odd, two[1], two[0]))
            sources.append(swap(jnp.where(odd, two[0], two[1]), "win", 1))
        left = call(
            lambda *refs: source_kernel(nbins, windows, *refs),
            jax.ShapeDtypeStruct((4 * n_grp, share * K8, 3 * chans // 2), jnp.bfloat16),
            sources,
            [
                pltpu.VMEM((n_grp * K16 + 2 * K8, chans), jnp.float32),
                pltpu.VMEM((n_grp, 3 * K16, chans), jnp.float32),
                pltpu.VMEM((share * K8, 2 * share), jnp.bfloat16),
            ],
            "sources",
            [vmem] * 4,
            grid=(n_grp,),
            out_specs=pl.BlockSpec((4, share * K8, 3 * chans // 2), lambda i: (i, 0, 0)),
        )
        core_far = swap(after(far_2, left, over_2), "win", 1)
        over_3 = swap(after(got_3, core_far), "win", 2)
        held = {(r, d): r for r in range(2) for d in range(2)}
        if case < 2:
            held |= {(one, d): 0 for d in (2, 3)} | {(other, d): 1 for d in (2, 3)}
        else:
            held |= {(r, 2): r for r in range(2)} | {(r, 3): 1 - r for r in range(2)}
        spots = [[(0, 0), (4, 0), (2, 0), (4, 4)], [(1, 0), (4, 2), (3, 0), (4, 6)]]
        spots += [[(0, 0), (4, 0), (2, 0), (5, 2)], [(1, 0), (5, 0), (3, 0), (6, 0)]]

        def places_of(phase):
            kinds = [(r, d) for r in range(ROUNDS) for d in (2 * phase, 2 * phase + 1)]
            return [[(spots[d][e][0], spots[d][e][1] + held[r, d]) for r, d in kinds] for e in range(4)]

        early_pieces = [own, near_2, over_0, over_1]
        early_pieces.append(swap(after(jnp.concatenate(early_pieces, axis=0), got_b), "win", 1))
        lag = jnp.asarray(lag_matrix(nbins))
        taken = [
            pltpu.VMEM((n_grp, 2, 2, 24, K8, chans), jnp.float32),
            pltpu.VMEM((n_grp * K16 + 2 * K8, chans), jnp.float32),
            pltpu.VMEM((n_grp, 2, 2, K8, chans), jnp.float32),
        ]
        early_places = places_of(0)
        early = call(
            lambda *refs: receive_kernel(early_places, nbins, windows, *refs),
            jax.ShapeDtypeStruct((4 * n_grp, 24 * K8, chans), jnp.bfloat16),
            (here, *early_pieces),
            taken,
            "receivers",
            [smem] + [vmem] * len(early_pieces),
        )
        late_places = places_of(1)
        late_pieces = [far_2, got_3, over_2, over_3, core_far]
        late_pieces.append(swap(jnp.concatenate([got_3, over_2], axis=0), "win", 1))
        late_pieces.append(swap(after(over_3, early), "win", 1))
        hbm = pl.BlockSpec(memory_space=pl.ANY)
        by_lag = call(
            lambda *refs: correlate_kernel(late_places, nbins, windows, *refs),
            jax.ShapeDtypeStruct((ROUNDS, L, share, chans), jnp.bfloat16),
            (here, left, early, lag, *late_pieces),
            [
                pltpu.VMEM(left.shape, jnp.bfloat16),
                pltpu.VMEM(early.shape, jnp.bfloat16),
                taken[0],
                pltpu.VMEM((share, n_grp * 4 * K8, ROUNDS * chans), jnp.bfloat16),
                pltpu.VMEM((ROUNDS, lag.shape[0] * share, chans), jnp.float32),
                *taken[1:],
                pltpu.SemaphoreType.DMA((2,)),
            ],
            "correlate",
            [smem, hbm, hbm] + [vmem] * (1 + len(late_pieces)),
        )
        return by_lag.transpose(0, 2, 1, 3)

    return branch


def gathering_body(spectra, channel_slot, partners):
    here = lax.axis_index("blk")
    masks = partners[:, 0]
    case = jnp.where(masks[0] == 1, 0, jnp.where(masks[1] == 1, 1, 2))
    branches = [make_branch(i) for i in range(3)]
    return lax.switch(case, branches, spectra, channel_slot, partners, here.reshape(1))


def solution(mesh):
    in_specs = (P(None, "win", ("groups", "blk"), None), P(("groups", "blk")), P())
    out_specs = P(None, ("groups", "blk", "win"), None, None)

    def body(spectra, channel_slot, partners):
        small = all((mesh.shape[axis] - 1).bit_length() == 2 for axis in ("blk", "win"))
        small = small and spectra.shape[2] == LANES and spectra.shape[1] // 2 == 3 and spectra.shape[3] <= 2 * LANES
        return (gathering_body if small else walking_body)(spectra, channel_slot, partners)

    return jax.shard_map(body, mesh=mesh, in_specs=in_specs, out_specs=out_specs, check_vma=False)
```

```python
import math

import jax
import jax.numpy as jnp
import numpy as np
from jax import lax
from jax.experimental import pallas as pl
from jax.experimental.pallas import tpu as pltpu
from jax.sharding import PartitionSpec as P

L = 101
ROUNDS = 2

eps_power = 1e-06
half_band = 2
tile_rows = 8
LANES = 128
K8 = 8
K16 = 16
K4 = 4
MIB = 2**20


def shortened(value):

    def short(part):
        return part.astype(jnp.bfloat16) if part.dtype == jnp.float32 else part

    return jax.tree.map(short, value)


def partner(value, axis, distance):
    mask = 2**distance
    pairs = [(source, source ^ mask) for source in range(lax.axis_size(axis))]
    return lax.ppermute(value, axis, pairs)


def band_mean(power, windows):
    nbins = power.shape[1]
    padded = jnp.pad(power, ((0, 0), (half_band, half_band)))
    ones = jnp.pad(jnp.ones((nbins,), jnp.float32), (half_band, half_band))
    total = padded[:, 0:nbins]
    count = ones[0:nbins]
    for offset in range(1, 2 * half_band + 1):
        total = total + padded[:, offset : offset + nbins]
        count = count + ones[offset : offset + nbins]
    return total / (count * windows)


def power_of(parts):
    value_array = parts.astype(jnp.float32)
    return jnp.sum(value_array * value_array, axis=(0, 1))


def whiten(parts, power, windows):
    scale = lax.rsqrt(band_mean(power, windows) + eps_power)
    return (parts.astype(jnp.float32) * scale).astype(jnp.bfloat16)


def lag_table(nbins, nlags, windows):
    samples = 2 * (nbins - 1)
    freq = jnp.arange(nbins, dtype=jnp.int32)
    lags = jnp.arange(nlags, dtype=jnp.int32) - (nlags - 1) // 2
    phase_index = freq[:, None] * lags[None, :] % samples
    angle = 2.0 * math.pi / samples * phase_index.astype(jnp.float32)
    weight = jnp.where((freq == 0) | (freq == nbins - 1), 1.0, 2.0).astype(jnp.float32)
    norm = 1.0 / math.sqrt(windows * samples)
    cos_part = weight[:, None] * jnp.cos(angle) * norm
    sin_part = -weight[:, None] * jnp.sin(angle) * norm
    return jnp.concatenate([cos_part, sin_part], axis=0)


def correlate(sources, receivers, table):
    left = jnp.concatenate([sources[0], sources[1]], axis=0)
    turned = jnp.concatenate([sources[1], -sources[0]], axis=0)
    right = jnp.concatenate([receivers[0], receivers[1]], axis=0)
    count = left.shape[1] // tile_rows

    def one_tile(index):
        start = index * tile_rows
        part_left = lax.dynamic_slice_in_dim(left, start, tile_rows, 1)
        part_turned = lax.dynamic_slice_in_dim(turned, start, tile_rows, 1)
        real = jnp.einsum("wak,wbk->kab", part_left, right, preferred_element_type=jnp.float32)
        imag = jnp.einsum("wak,wbk->kab", part_turned, right, preferred_element_type=jnp.float32)
        stacked = jnp.concatenate([real, imag], axis=0)
        return jnp.einsum("kab,kl->alb", stacked, table, precision=lax.Precision.HIGHEST)

    result = lax.map(one_tile, jnp.arange(count, dtype=jnp.int32))
    return result.reshape(count * tile_rows, table.shape[1], right.shape[1]).astype(jnp.bfloat16)


def make_walker(mask_bits, depth):

    def walker(moving):
        for bit in range(depth):
            if mask_bits >> bit & 1:
                moving = jax.tree.map(
                    lambda part, own: part.astype(own.dtype),
                    partner(shortened(moving), "blk", bit),
                    moving,
                )
        return moving

    return walker


def walking_body(spectra, channel_slot, partners):
    n_blk = lax.axis_size("blk")
    n_win = lax.axis_size("win")
    chans = spectra.shape[2]
    nbins = spectra.shape[3]
    per_peer = chans // n_blk
    here = lax.axis_index("blk")
    target = channel_slot // chans * per_peer + channel_slot % chans - here * per_peer
    selector = (jnp.arange(chans, dtype=jnp.int32)[:, None] == target[None, :]).astype(jnp.bfloat16)
    ordered = jnp.einsum(
        "pc,rwcf->rwpf", selector, spectra, preferred_element_type=jnp.float32
    ).astype(jnp.bfloat16)
    blocked = lax.all_to_all(ordered, "blk", split_axis=2, concat_axis=2, tiled=True)
    windows = spectra.shape[1] * n_win
    power = lax.psum(power_of(blocked), "win")
    outgoing = whiten(blocked, power, windows)
    own_all = lax.all_gather(outgoing, "win", axis=1, tiled=True)
    share = chans // n_win
    sources = lax.dynamic_slice_in_dim(own_all, lax.axis_index("win") * share, share, 2)
    table = lag_table(nbins, L, windows)
    masks = jnp.bitwise_xor(partners[:, here], here)
    bits = n_blk.bit_length() - 1
    results = []
    walkers = [make_walker(mask_bits, bits) for mask_bits in range(1, n_blk)]
    for round_index in range(ROUNDS):
        moving = lax.switch(masks[round_index] - 1, walkers, outgoing)
        partner_all = jax.tree.map(
            lambda part, own: part.astype(own.dtype),
            lax.all_gather(shortened(moving), "win", axis=1, tiled=True),
            moving,
        )
        results.append(correlate(sources, partner_all, table))
    return jnp.stack(results, axis=0)


def iota(shape, dim):
    return lax.broadcasted_iota(jnp.int32, shape, dim)


def bins_of(nbins):
    return -(-nbins // K16)


def lag_matrix(nbins):
    samples = 2 * (nbins - 1)
    groups = 2 * bins_of(nbins)
    rows = -(-L // K8) * K8
    freq = np.arange(nbins)
    lags = np.arange(L) - (L - 1) // 2
    angle = 2.0 * np.pi / samples * (freq[:, None] * lags[None, :] % samples)
    weight = np.where((freq == 0) | (freq == nbins - 1), 1.0, 2.0)[:, None]
    full = np.zeros((rows, 2, groups * K8))
    full[:L, 0, :nbins] = (weight * np.cos(angle)).T
    full[:L, 1, :nbins] = -(weight * np.sin(angle)).T
    full = full.reshape(rows, 2, 2 * groups, K4).transpose(0, 2, 1, 3).reshape(rows, groups * 2 * K8)
    return full.astype(jnp.bfloat16)


def top(shape):
    return iota(shape, 0) % K8 < K4


def moved_by(value, rows):
    return pltpu.roll(value, rows % value.shape[0], 0)


def low_rows(first, second):
    return jnp.where(top(first.shape), first, moved_by(second, K4))


def high_rows(first, second):
    return jnp.where(top(first.shape), moved_by(first, -K4), second)


def tiles_of(first, second, third):
    return low_rows(first, second), third, high_rows(first, second)


def bins_from(tiles):
    low, both, high = tiles
    rest = jnp.where(top(low.shape), low + moved_by(low, -K4), high + moved_by(high, K4))
    return both + rest


def pack_kernel(layout, nbins, here_ref, part_ref, slot_ref, x_ref, *rest):
    outs, (wide_ref, blocks_ref) = rest[: len(layout)], rest[len(layout) :]
    n_blk, n_grp, n_row, lanes = blocks_ref.shape
    per_peer = lanes // 4
    chans = slot_ref.shape[1]
    here = here_ref[0]
    slot = slot_ref[...]
    target = slot // chans * per_peer + slot % chans - here * per_peer
    shape = (n_blk * lanes, chans)
    row = iota(shape, 0)
    pick = jnp.where(target == row // lanes * per_peer + row % per_peer, 1.0, 0.0).astype(jnp.bfloat16)
    rows = math.prod(x_ref.shape[:-1])
    wide = lax.dot_general(x_ref[...].reshape(rows, chans), pick, (((1,), (1,)), ((), ())), preferred_element_type=jnp.float32)
    for block in range(n_blk):
        wide_ref[block, pl.ds(0, rows), :] = wide[:, block * lanes : (block + 1) * lanes]
    bins = n_grp * K16
    lane_group = iota((bins, lanes), 1) // per_peer
    inside = iota((bins, lanes), 0) < nbins
    for block in range(n_blk):
        values = []
        for pair in range(3):
            value = jnp.zeros((bins, lanes), jnp.float32)
            for g in range(4):
                start = (2 * pair + g % 2) * 2 * nbins + g // 2
                value = jnp.where(lane_group == g, wide_ref[block, pl.ds(start, bins, stride=2), :], value)
            values.append(jnp.where(inside, value, 0.0))
        tiles = [tile.reshape(n_grp, 2, 1, K8, lanes) for tile in tiles_of(*values)]
        blocks_ref[block] = jnp.concatenate(tiles, axis=2).reshape(n_grp, n_row, lanes).astype(jnp.bfloat16)
    masks = [part_ref[r, here] ^ here for r in range(ROUNDS)]
    masks.append(masks[0] ^ masks[1])
    for out, message in zip(outs, layout):
        for place, (step, name) in enumerate(message):
            mask = 0 if name is None else masks[name]
            out[place] = blocks_ref[here ^ step ^ mask]


def scale_of(power_ref, nbins, windows):
    rows = power_ref.shape[0] - 2 * K8
    total = power_ref[pl.ds(K8 - half_band, rows), :]
    for offset in range(1, 2 * half_band + 1):
        total = total + power_ref[pl.ds(K8 - half_band + offset, rows), :]
    bin_ = iota(total.shape, 0)
    count = jnp.minimum(bin_ + half_band, nbins - 1) - jnp.maximum(bin_ - half_band, 0) + 1
    count = jnp.maximum(count, 1).astype(jnp.float32)
    return lax.rsqrt(total / (count * windows) + eps_power)


def source_kernel(nbins, windows, *refs):
    src, (out_ref, power_ref, scale_ref, copies_ref) = refs[:4], refs[4:]
    n_grp, n_row, lanes = src[0].shape[1:]
    share = lanes // 4
    step = pl.program_id(0)

    @pl.when(step == 0)
    def _():
        totals = [jnp.zeros((n_grp, 2, K8, lanes), jnp.float32) for _ in range(3)]
        for ref in src:
            value = ref[0].astype(jnp.float32).reshape(n_grp, 2, 3, K8, lanes)
            totals = [total + value[:, :, i] * value[:, :, i] for i, total in enumerate(totals)]
        total = bins_from([total.reshape(n_grp * K16, lanes) for total in totals])
        total = total + pltpu.roll(total, 2 * share, 1)
        total = total + pltpu.roll(total, share, 1)
        power_ref[...] = jnp.zeros(power_ref.shape, jnp.float32)
        power_ref[pl.ds(K8, n_grp * K16), :] = total
        scale = scale_of(power_ref, nbins, windows)
        scales = [low_rows(scale, scale), scale, high_rows(scale, scale)]
        scales = [value.reshape(n_grp, 2, 1, K8, lanes) for value in scales]
        scale_ref[...] = jnp.concatenate(scales, axis=2).reshape(scale_ref.shape)
        row, col = iota(copies_ref.shape, 0), iota(copies_ref.shape, 1)
        same = (col % share == row // K8) & (col // share == row // K4 % 2)
        copies_ref[...] = jnp.where(same, 1.0, 0.0).astype(jnp.bfloat16)

    scale = scale_ref[step]
    white = [(ref[0, step].astype(jnp.float32) * scale).astype(jnp.bfloat16).astype(jnp.float32) for ref in src]
    lane = iota((share, lanes), 1)
    shape = (copies_ref.shape[0], 2 * lanes)
    keep = iota(shape, 0) % K4 == iota(shape, 1) % K4
    for half in range(2):
        tiles = [[value[(3 * half + i) * K8 : (3 * half + i + 1) * K8] for value in white] for i in range(3)]
        third = tiles[1]
        rows = tiles[0] + [low_rows(third[0], third[1]), low_rows(third[2], third[3])]
        rows = rows + tiles[2] + [high_rows(third[0], third[1]), high_rows(third[2], third[3])]
        width = len(rows) * K4
        rows = rows + [jnp.zeros((lanes - len(rows) * K8, lanes), jnp.float32)]
        turned = jnp.concatenate(rows, axis=0).T
        by_group = [turned[g * share : (g + 1) * share] for g in range(4)]
        crossed = [by_group[2], by_group[3], -by_group[0], -by_group[1]]
        for group in range(2):
            lines = []
            for values in (by_group, crossed):
                for start, size in ((0, 8 * K4), (8 * K4, 4 * K4)):
                    line = jnp.zeros((share, lanes), jnp.float32)
                    for g in range(4):
                        shift = (g * size - group * width - start) % lanes
                        moved = pltpu.roll(values[g], shift, 1) if shift else values[g]
                        line = jnp.where(lane // size == g, moved, line)
                    lines.append(line)
            lines = jnp.concatenate(
                [jnp.concatenate(lines[:2], axis=1), jnp.concatenate(lines[2:], axis=1)], axis=0
            ).astype(jnp.bfloat16)
            spread = jnp.dot(copies_ref[...], lines, preferred_element_type=jnp.float32)
            spread = jnp.where(keep, spread, 0.0).astype(jnp.bfloat16)
            out_ref[2 * half + group] = spread[:, : out_ref.shape[2]]


def take_pieces(pieces, places, phase, here, right_ref, power_ref, scale_ref, nbins, windows):
    n_grp, n_row, lanes = pieces[0].shape[1:]
    share = lanes // 4
    shape = (4 * lanes, 4 * lanes)
    row, col = iota(shape, 0), iota(shape, 1)
    kind = row // lanes
    half = (here >> 1) ^ phase ^ (kind >> 1)
    odd = (here ^ kind) & 1
    spot = row % lanes // share * lanes + (2 * half + odd) * share + row % share
    order = jnp.where(col == spot, 1.0, 0.0).astype(jnp.bfloat16)
    flat, tall = (n_grp * K16, lanes), (n_grp, 2, K8, lanes)
    totals = [jnp.zeros(tall, jnp.float32) for _ in range(3)]
    before = [None] * 4
    for e in range(4):
        parts = [pieces[operand][index].reshape(n_grp * n_row, lanes) for operand, index in places[e]]
        moved = jnp.dot(jnp.concatenate(parts, axis=1), order, preferred_element_type=jnp.float32)
        moved = moved.reshape(n_grp, 2, 3, K8, 4 * lanes)
        for g in range(4):
            low, both, high = values = [moved[:, :, i, :, g * lanes : (g + 1) * lanes] for i in range(3)]
            totals = [total + value * value for total, value in zip(totals, values)]
            right_ref[:, :, 0, g * 4 + e] = low
            right_ref[:, :, 1, g * 4 + e] = high
            both = both.reshape(flat)
            if e % 2:
                spot = 16 + g * 2 + e // 2
                right_ref[:, :, 0, spot] = low_rows(before[g], both).reshape(tall)
                right_ref[:, :, 1, spot] = high_rows(before[g], both).reshape(tall)
            before[g] = both
    power_ref[...] = jnp.zeros(power_ref.shape, jnp.float32)
    power_ref[pl.ds(K8, n_grp * K16), :] = bins_from([total.reshape(flat) for total in totals])
    scale = scale_of(power_ref, nbins, windows)
    scale_ref[:, :, 0] = low_rows(scale, scale).reshape(tall)
    scale_ref[:, :, 1] = high_rows(scale, scale).reshape(tall)


def whitened(right_ref, scale_ref, index, half, group):
    white = (right_ref[index, half, group] * scale_ref[index, half, group]).astype(jnp.bfloat16)
    return white.reshape(-1, white.shape[-1])


def receive_kernel(places, nbins, windows, here_ref, *rest):
    pieces, (out_ref, right_ref, power_ref, scale_ref) = rest[:-4], rest[-4:]
    take_pieces(pieces, places, 0, here_ref[0], right_ref, power_ref, scale_ref, nbins, windows)

    def one_group(index, carry):
        for half in range(2):
            for group in range(2):
                out_ref[4 * index + 2 * half + group] = whitened(right_ref, scale_ref, index, half, group)
        return carry

    lax.fori_loop(0, right_ref.shape[0], one_group, 0)


def correlate_kernel(places, nbins, windows, here_ref, left_hbm, early_hbm, lag_ref, *rest):
    pieces, rest = rest[:-9], rest[-9:]
    out_ref, left_ref, early_ref, right_ref, cross_ref, lagged_ref, power_ref, scale_ref, sems = rest
    copies = [
        pltpu.make_async_copy(left_hbm, left_ref, sems.at[0]),
        pltpu.make_async_copy(early_hbm, early_ref, sems.at[1]),
    ]
    for copy in copies:
        copy.start()
    here = here_ref[0]
    take_pieces(pieces, places, 1, here, right_ref, power_ref, scale_ref, nbins, windows)
    for copy in copies:
        copy.wait()

    def one_group(index, carry):
        for half in range(2):
            crosses = []
            for group in range(2):
                spot = 4 * index + 2 * half + group
                both = jnp.concatenate([early_ref[spot], whitened(right_ref, scale_ref, index, half, group)], axis=1)
                cross = jnp.dot(left_ref[spot], both, preferred_element_type=jnp.float32)
                crosses.append(cross.reshape(-1, K8, cross.shape[-1]))
            place = pl.multiple_of((2 * index + half) * K16, K16)
            cross_ref[:, pl.ds(place, K16), :] = jnp.concatenate(crosses, axis=1).astype(jnp.bfloat16)
        return carry

    lax.fori_loop(0, right_ref.shape[0], one_group, 0, unroll=True)
    norm = 1.0 / math.sqrt(windows * 2 * (nbins - 1))
    share, lanes = cross_ref.shape[0], pieces[0].shape[-1]
    first = iota((lag_ref.shape[0], lanes), 1) // (2 * share) == here >> 1

    def one_source(index, carry):
        lagged = jnp.dot(lag_ref[...], cross_ref[index], preferred_element_type=jnp.float32) * norm
        early, late = lagged[:, :lanes], lagged[:, lanes:]
        rounds = [jnp.where(first, early, late), pltpu.roll(jnp.where(first, late, early), lanes // 2, 1)]
        for r in range(ROUNDS):
            lagged_ref[r, pl.ds(index, lagged.shape[0], stride=share), :] = rounds[r]
        return carry

    lax.fori_loop(0, share, one_source, 0, unroll=True)
    for r in range(ROUNDS):
        out_ref[r] = lagged_ref[r, pl.ds(0, L * share), :].astype(jnp.bfloat16).reshape(L, share, lanes)


def swap(value, axis, mask):
    return lax.ppermute(value, axis, [(i, i ^ mask) for i in range(lax.axis_size(axis))])


def call(kernel, outs, operands, scratch, name, specs=None, vmem_mib=40, **grid):
    return pl.pallas_call(
        kernel,
        cost_estimate=pl.CostEstimate(flops=0, bytes_accessed=MIB, transcendentals=0),
        out_shape=outs,
        in_specs=specs,
        scratch_shapes=scratch,
        compiler_params=pltpu.CompilerParams(vmem_limit_bytes=vmem_mib * MIB),
        name=name,
        **grid,
    )(*operands)


def after(value, *earlier):
    return lax.optimization_barrier((value, *earlier))[0]


def make_branch(case):
    one, other = (case, 1 - case) if case < 2 else (None, None)

    def branch(spectra, channel_slot, partners, here):
        chans, nbins = spectra.shape[2:]
        windows = spectra.shape[1] * lax.axis_size("win")
        n_grp = bins_of(nbins)
        share = chans // 4
        piece = (n_grp, 3 * K16, chans)
        win = lax.axis_index("win")
        layout = [[(3, None), (2, None)], [(2, 2), (2, other)] if case < 2 else [(2, 0), (2, 1)]]
        layout += [[(1, 0), (1, 1), (1, None)], [(0, 0), (0, 1)], [(0, None)]]
        vmem, smem = pl.BlockSpec(memory_space=pltpu.VMEM), pl.BlockSpec(memory_space=pltpu.SMEM)
        far_a, far_b, near, own, own_src = call(
            lambda *refs: pack_kernel(layout, nbins, *refs),
            [jax.ShapeDtypeStruct((len(m),) + piece, jnp.bfloat16) for m in layout],
            (here, partners, channel_slot.reshape(1, chans), spectra.transpose(1, 3, 0, 2)),
            [
                pltpu.VMEM((4, spectra.shape[1] * 2 * nbins + 4 * K16, chans), jnp.float32),
                pltpu.VMEM((4,) + piece, jnp.bfloat16),
            ],
            "pack",
            [smem, smem, vmem, vmem],
        )
        z = here[0]
        mine = (z >> 1) == (win >> 1)
        got_1 = swap(near, "blk", 1)
        got_a = swap(far_a, "blk", 2)
        got_b = swap(after(far_b, got_a), "blk", 2)
        over_0 = swap(own, "win", 2)
        near_2, far_2, passed = got_1[:2], got_b, got_b
        if case < 2:
            far_2 = jnp.concatenate([got_a[:1], got_b[1:]], axis=0)
            passed = jnp.concatenate([got_a[1:], got_b[:1]], axis=0)
        over_1 = swap(after(near_2, over_0), "win", 2)
        got_src = swap(got_a[:1], "blk", 1)
        over_2 = swap(far_2, "win", 2)
        src = [own_src, got_1[2:], got_a[1:], after(got_src, over_1)]
        high = [jnp.where(mine, src[d + 2], src[d]) for d in range(2)]
        across = swap(jnp.concatenate(high, axis=0), "win", 2)
        low = [jnp.where(mine, src[d], src[d + 2]) for d in range(2)]
        got_3 = swap(after(passed, over_1, across), "blk", 1)
        odd = ((win ^ z) & 1) == 1
        first, second = low, [across[0:1], across[1:2]]
        sources = []
        for two in (first, second):
            sources.append(jnp.where(odd, two[1], two[0]))
            sources.append(swap(jnp.where(odd, two[0], two[1]), "win", 1))
        left = call(
            lambda *refs: source_kernel(nbins, windows, *refs),
            jax.ShapeDtypeStruct((4 * n_grp, share * K8, 3 * chans // 2), jnp.bfloat16),
            sources,
            [
                pltpu.VMEM((n_grp * K16 + 2 * K8, chans), jnp.float32),
                pltpu.VMEM((n_grp, 3 * K16, chans), jnp.float32),
                pltpu.VMEM((share * K8, 2 * share), jnp.bfloat16),
            ],
            "sources",
            [vmem] * 4,
            grid=(n_grp,),
            out_specs=pl.BlockSpec((4, share * K8, 3 * chans // 2), lambda i: (i, 0, 0)),
        )
        core_far = swap(after(far_2, left, over_2), "win", 1)
        over_3 = swap(after(got_3, core_far), "win", 2)
        held = {(r, d): r for r in range(2) for d in range(2)}
        if case < 2:
            held |= {(one, d): 0 for d in (2, 3)} | {(other, d): 1 for d in (2, 3)}
        else:
            held |= {(r, 2): r for r in range(2)} | {(r, 3): 1 - r for r in range(2)}
        spots = [[(0, 0), (4, 0), (2, 0), (4, 4)], [(1, 0), (4, 2), (3, 0), (4, 6)]]
        spots += [[(0, 0), (4, 0), (2, 0), (5, 2)], [(1, 0), (5, 0), (3, 0), (6, 0)]]

        def places_of(phase):
            kinds = [(r, d) for r in range(ROUNDS) for d in (2 * phase, 2 * phase + 1)]
            return [[(spots[d][e][0], spots[d][e][1] + held[r, d]) for r, d in kinds] for e in range(4)]

        early_pieces = [own, near_2, over_0, over_1]
        early_pieces.append(swap(after(jnp.concatenate(early_pieces, axis=0), got_b), "win", 1))
        lag = jnp.asarray(lag_matrix(nbins))
        taken = [
            pltpu.VMEM((n_grp, 2, 2, 24, K8, chans), jnp.float32),
            pltpu.VMEM((n_grp * K16 + 2 * K8, chans), jnp.float32),
            pltpu.VMEM((n_grp, 2, 2, K8, chans), jnp.float32),
        ]
        early_places = places_of(0)
        early = call(
            lambda *refs: receive_kernel(early_places, nbins, windows, *refs),
            jax.ShapeDtypeStruct((4 * n_grp, 24 * K8, chans), jnp.bfloat16),
            (here, *early_pieces),
            taken,
            "receivers",
            [smem] + [vmem] * len(early_pieces),
        )
        late_places = places_of(1)
        late_pieces = [far_2, got_3, over_2, over_3, core_far]
        late_pieces.append(swap(jnp.concatenate([got_3, over_2], axis=0), "win", 1))
        late_pieces.append(swap(after(over_3, early), "win", 1))
        hbm = pl.BlockSpec(memory_space=pl.ANY)
        by_lag = call(
            lambda *refs: correlate_kernel(late_places, nbins, windows, *refs),
            jax.ShapeDtypeStruct((ROUNDS, L, share, chans), jnp.bfloat16),
            (here, left, early, lag, *late_pieces),
            [
                pltpu.VMEM(left.shape, jnp.bfloat16),
                pltpu.VMEM(early.shape, jnp.bfloat16),
                taken[0],
                pltpu.VMEM((share, n_grp * 4 * K8, ROUNDS * chans), jnp.bfloat16),
                pltpu.VMEM((ROUNDS, lag.shape[0] * share, chans), jnp.float32),
                *taken[1:],
                pltpu.SemaphoreType.DMA((2,)),
            ],
            "correlate",
            [smem, hbm, hbm] + [vmem] * (1 + len(late_pieces)),
        )
        return by_lag.transpose(0, 2, 1, 3)

    return branch


def gathering_body(spectra, channel_slot, partners):
    here = lax.axis_index("blk")
    masks = partners[:, 0]
    case = jnp.where(masks[0] == 1, 0, jnp.where(masks[1] == 1, 1, 2))
    branches = [make_branch(i) for i in range(3)]
    return lax.switch(case, branches, spectra, channel_slot, partners, here.reshape(1))


def solution(mesh):
    in_specs = (P(None, "win", ("groups", "blk"), None), P(("groups", "blk")), P())
    out_specs = P(None, ("groups", "blk", "win"), None, None)

    def body(spectra, channel_slot, partners):
        small = all((mesh.shape[axis] - 1).bit_length() == 2 for axis in ("blk", "win"))
        small = small and spectra.shape[2] == LANES and spectra.shape[1] // 2 == 3 and spectra.shape[3] <= 2 * LANES
        return (gathering_body if small else walking_body)(spectra, channel_slot, partners)

    return jax.shard_map(body, mesh=mesh, in_specs=in_specs, out_specs=out_specs, check_vma=False)
```
